32 devices in a mesh: tm: 16 (over z, x, core), chan: 2 (over y).
Axes of the slice: x: 2, y: 2, z: 4, core: 2. Of those that a mesh axis runs over, the one named last changes fastest.
Arguments:
- features: bfloat16 [512, 64, 128], P('chan', 'tm'), may hold values from -6 to 6
- gain_one: float32 [512], replicated, may hold values from 0.1 to 1.9
- shift_one: float32 [512], replicated, may hold values from -3 to 3
- conv_one: bfloat16 [27, 512, 512], P(None, None, 'chan'), may hold values from -0.0546875 to 0.0546875
- bias_one: float32 [512], P('chan'), may hold values from -3 to 3
- gain_two: float32 [512], replicated, may hold values from 0.1 to 1.9
- shift_two: float32 [512], replicated, may hold values from -3 to 3
- conv_two: bfloat16 [27, 512, 256], P(None, None, 'chan'), may hold values from -0.0546875 to 0.0546875
- cotangent: bfloat16 [256, 128, 512], P('chan', 'tm'), may hold values from -6 to 6
- frame_weight: int32 [128], P('tm'), may hold values from 0 to 4
Outputs:
- grad_features: bfloat16 [512, 64, 128], P('chan', 'tm')
The draws below stay inside these ranges and needn't reach their ends.
All inputs are finite; a program needn't handle non-finite values.
Results may differ from the reference program's by a relative error of at most 0.0075.
Values may be sent and summed in bfloat16 or wider, within the bound.
A program may use at most 192 MiB of HBM per device.

```python
import jax
import jax.numpy as jnp
from jax import lax

C1 = 512
C2 = 256
GROUPS = 32
H1 = 8
W1 = 16
T1 = 64
T2 = 128


def draw_cotangent(key, part):
    key = jax.random.fold_in(key, 11)
    key_offset, key_noise = jax.random.split(key, 2)
    shape = (C2, T2, 4 * H1 * W1)
    offset = jax.random.uniform(key_offset, (C2, 1, 1), jnp.float32, 0.5, 1.5)
    values = jax.random.normal(key_noise, shape, jnp.float32) + offset
    return jnp.clip(values, -6.0, 6.0).astype(jnp.bfloat16)


def touch_ends(entries, rng, low, top_value):
    longest = entries.shape.index(max(entries.shape))
    spots = []
    for shift in (0, 1):
        where = [jax.random.randint(jax.random.fold_in(rng, axis), (), 0, length) for axis, length in enumerate(entries.shape)]
        where[longest] = (where[longest] + shift) % entries.shape[longest]
        spots.append(tuple(where))
    return entries.at[spots[0]].set(low).at[spots[1]].set(top_value)


def level_of(stream_key, extent, cuts, smallest, top_value):
    def one(position, blocks):
        steps = jax.random.uniform(jax.random.fold_in(jax.random.fold_in(stream_key, 6), position), (blocks,), jnp.float32, smallest / len(cuts), top_value / len(cuts))
        return jnp.repeat(jnp.exp(steps), extent[position] // blocks).reshape((-1,) + (1,) * (len(extent) - position - 1))

    level = one(*cuts[0])
    for cut in cuts[1:]:
        level = level * one(*cut)
    return level


def scatter_about(rng, shape, scale, limit, cuts=(), held_as=jnp.bfloat16):
    level = level_of(rng, shape, cuts, -0.22, 0.18) if cuts else 1.0
    drawn = jax.random.normal(rng, shape, jnp.float32) * scale * level
    return jnp.minimum(jnp.maximum(drawn, -limit), limit).astype(held_as)


def setup_inputs(seed: int = 0) -> dict:
    key_list = jax.random.split(jax.random.key(seed), 11)
    features = scatter_about(key_list[0], (C1, T1, H1 * W1), 1.0, 6.0, ((0, 2), (1, 16)))
    gain_one = jnp.clip(1.0 + 0.18 * jax.random.normal(key_list[1], (C1,), jnp.float32), 0.1, 1.9)
    shift_one = scatter_about(key_list[2], (C1,), 0.5, 3.0, (), jnp.float32)
    conv_one = scatter_about(key_list[3], (27, C1, C1), (27 * C1) ** -0.5, 0.0546875, ((2, 2),))
    bias_one = scatter_about(key_list[4], (C1,), 0.5, 3.0, ((0, 2),), jnp.float32)
    gain_two = jnp.clip(1.0 + 0.18 * jax.random.normal(key_list[5], (C1,), jnp.float32), 0.1, 1.9)
    shift_two = scatter_about(key_list[6], (C1,), 0.5, 3.0, (), jnp.float32)
    conv_two = scatter_about(key_list[7], (27, C1, C2), (27 * C1) ** -0.5, 0.0546875, ((2, 2),))
    cotangent = draw_cotangent(jax.random.fold_in(key_list[10], 71), 0)
    frame_weight = touch_ends(jax.random.randint(key_list[9], (T2,), 0, 5), jax.random.fold_in(key_list[9], 1), 0, 4).astype(jnp.int32)
    return dict(features=features, gain_one=gain_one, shift_one=shift_one, conv_one=conv_one, bias_one=bias_one, gain_two=gain_two, shift_two=shift_two, conv_two=conv_two, cotangent=cotangent, frame_weight=frame_weight)


EPS = 1e-06

def spatial_shift(values, height, width, delta_y, delta_x):
    lead = values.shape[:-1]
    grid = values.reshape(lead + (height, width))
    pads = [(0, 0)] * len(lead) + [(1, 1), (1, 1)]
    grid = jnp.pad(grid, pads)
    piece = grid[..., 1 + delta_y:1 + delta_y + height, 1 + delta_x:1 + delta_x + width]
    return piece.reshape(lead + (height * width,))

def conv_forward(extended, weight, height, width):
    frames = extended.shape[1] - 2
    total = jnp.zeros((weight.shape[2], frames, extended.shape[2]), jnp.float32)
    for tap in range(9):
        moved = spatial_shift(extended, height, width, tap // 3 - 1, tap % 3 - 1).astype(jnp.float32)
        for depth in range(3):
            total = total + jnp.einsum('cts,co->ots', moved[:, depth:depth + frames], weight[depth * 9 + tap].astype(jnp.float32))
    return total

def conv_transpose(extended, weight, height, width):
    frames = extended.shape[1] - 2
    total = jnp.zeros((weight.shape[1], frames, extended.shape[2]), jnp.float32)
    for tap in range(9):
        moved = spatial_shift(extended, height, width, 1 - tap // 3, 1 - tap % 3).astype(jnp.float32)
        for depth in range(3):
            total = total + jnp.einsum('ots,co->cts', moved[:, 2 - depth:2 - depth + frames], weight[depth * 9 + tap].astype(jnp.float32))
    return total

def group_norm(values, groups):
    grouped = values.reshape(groups, -1)
    mean = lax.optimization_barrier(jnp.mean(grouped, axis=1))
    centered = grouped - mean[:, None]
    inverse = jax.lax.rsqrt(lax.optimization_barrier(jnp.mean(centered * centered, axis=1)) + EPS)
    return ((centered * inverse[:, None]).reshape(values.shape), inverse)

def group_back(grad_norm, normed, inverse, groups):
    grads = grad_norm.reshape(groups, -1)
    norms = normed.reshape(groups, -1)
    first = lax.optimization_barrier(jnp.mean(grads, axis=1))
    second = lax.optimization_barrier(jnp.mean(grads * norms, axis=1))
    result = (grads - first[:, None] - norms * second[:, None]) * inverse[:, None]
    return result.reshape(grad_norm.shape)

def silu_slope(pre):
    sig = jax.nn.sigmoid(pre)
    return sig * (1.0 + pre * (1.0 - sig))

def reference(features, gain_one, shift_one, conv_one, bias_one, gain_two, shift_two, conv_two, cotangent, frame_weight):
    channels, frames_lo, cells = features.shape
    norm1, inv1 = group_norm(features.astype(jnp.float32), GROUPS)
    pre1 = norm1 * gain_one[:, None, None] + shift_one[:, None, None]
    act1 = jax.nn.silu(pre1).astype(jnp.bfloat16)
    before = jnp.zeros((channels, 2, cells), jnp.bfloat16)
    hidden = conv_forward(jnp.concatenate([before, act1], axis=1), conv_one, H1, W1)
    hidden = (hidden + bias_one[:, None, None]).astype(jnp.bfloat16)
    grid = hidden.reshape(channels, frames_lo, H1, W1)
    grid = jnp.repeat(jnp.repeat(jnp.repeat(grid, 2, axis=1), 2, axis=2), 2, axis=3)
    upsampled = grid.reshape(channels, 2 * frames_lo, 4 * cells)
    norm2, inv2 = group_norm(upsampled.astype(jnp.float32), GROUPS)
    pre2 = norm2 * gain_two[:, None, None] + shift_two[:, None, None]
    scale = frame_weight.astype(jnp.float32) / 4.0
    weighted = (cotangent.astype(jnp.float32) * scale[None, :, None]).astype(jnp.bfloat16)
    after = jnp.zeros((cotangent.shape[0], 2, cotangent.shape[2]), jnp.bfloat16)
    grad_act2 = conv_transpose(jnp.concatenate([weighted, after], axis=1), conv_two, 2 * H1, 2 * W1)
    grad_norm2 = grad_act2 * silu_slope(pre2) * gain_two[:, None, None]
    grad_up = group_back(grad_norm2, norm2, inv2, GROUPS)
    blocks = grad_up.reshape(channels, frames_lo, 2, H1, 2, W1, 2)
    grad_hidden = lax.optimization_barrier(jnp.sum(blocks, axis=(2, 4, 6))).reshape(channels, frames_lo, cells).astype(jnp.bfloat16)
    tail = jnp.zeros((channels, 2, cells), jnp.bfloat16)
    grad_act1 = conv_transpose(jnp.concatenate([grad_hidden, tail], axis=1), conv_one, H1, W1)
    grad_norm1 = grad_act1 * silu_slope(pre1) * gain_one[:, None, None]
    return group_back(grad_norm1, norm1, inv1, GROUPS).astype(jnp.bfloat16)
```

```python
import functools

import jax
import jax.numpy as jnp
from jax import lax
from jax.experimental import pallas as pl
from jax.experimental.pallas import tpu as pltpu
from jax.sharding import PartitionSpec as P

GROUPS = 32
H1 = 8
W1 = 16


EPS = 1e-06


def from_behind(block, axis, distance):
    devices = range(lax.axis_size(axis))
    route = [(i - distance, i) for i in devices if i - distance in devices]
    return lax.ppermute(block, axis, route)


def spatial_shift(values, height, width, delta_y, delta_x):
    lead = values.shape[:-1]
    grid = values.reshape(lead + (height, width))
    pads = [(0, 0)] * len(lead) + [(1, 1), (1, 1)]
    grid = jnp.pad(grid, pads)
    piece = grid[..., 1 + delta_y : 1 + delta_y + height, 1 + delta_x : 1 + delta_x + width]
    return piece.reshape(lead + (height * width,))


def conv_forward(extended, weight, height, width):
    frames = extended.shape[1] - 2
    moved = [spatial_shift(extended, height, width, tap // 3 - 1, tap % 3 - 1) for tap in range(9)]
    stacked = jnp.stack(
        [moved[tap][:, depth : depth + frames] for depth in range(3) for tap in range(9)], axis=0
    )
    return jnp.einsum("kcts,kco->ots", stacked, weight, preferred_element_type=jnp.float32)


def conv_transpose(extended, weight, height, width):
    frames = extended.shape[1] - 2
    moved = [spatial_shift(extended, height, width, 1 - tap // 3, 1 - tap % 3) for tap in range(9)]
    stacked = jnp.stack(
        [moved[tap][:, 2 - depth : 2 - depth + frames] for depth in range(3) for tap in range(9)],
        axis=0,
    )
    return jnp.einsum("kots,kco->cts", stacked, weight, preferred_element_type=jnp.float32)


def total_kernel(n, x_ref, o_ref, slots, send_sem, recv_sem):
    me = lax.axis_index("tm")
    barrier = pltpu.get_barrier_semaphore()
    for k in range(1, n):
        pl.semaphore_signal(
            barrier, inc=1, device_id={"tm": lax.rem(me + k, n)}, device_id_type=pl.DeviceIdType.MESH
        )
    pl.semaphore_wait(barrier, n - 1)
    copies = []
    for k in range(1, n):
        copy = pltpu.make_async_remote_copy(
            src_ref=x_ref,
            dst_ref=slots.at[k],
            send_sem=send_sem.at[k],
            recv_sem=recv_sem.at[k],
            device_id={"tm": lax.rem(me + k, n)},
            device_id_type=pl.DeviceIdType.MESH,
        )
        copy.start()
        copies.append(copy)
    for copy in copies:
        copy.wait()
    total = x_ref[...]
    for k in range(1, n):
        total = total + slots[k]
    o_ref[...] = total


def tm_total(values):
    n = lax.axis_size("tm")
    groups = values[0].shape[0]
    tile = jnp.pad(jnp.stack(values), ((0, 6), (0, 128 - groups)))
    out = pl.pallas_call(
        functools.partial(total_kernel, n),
        out_shape=jax.ShapeDtypeStruct((8, 128), jnp.float32),
        in_specs=[pl.BlockSpec(memory_space=pltpu.VMEM)],
        out_specs=pl.BlockSpec(memory_space=pltpu.VMEM),
        scratch_shapes=[
            pltpu.VMEM((n, 8, 128), jnp.float32),
            pltpu.SemaphoreType.DMA((n,)),
            pltpu.SemaphoreType.DMA((n,)),
        ],
        compiler_params=pltpu.CompilerParams(collective_id=0, has_side_effects=True),
    )(tile)
    return out[0, :groups], out[1, :groups]


def pooling(height, width):
    fine = lax.broadcasted_iota(jnp.int32, (4 * height * width, 9, height * width), 0)
    tap = lax.broadcasted_iota(jnp.int32, fine.shape, 1)
    cell = lax.broadcasted_iota(jnp.int32, fine.shape, 2)
    down = fine // (2 * width) - (2 * (cell // width) + 1 - tap // 3)
    across = fine % (2 * width) - (2 * (cell % width) + 1 - tap % 3)
    hit = (down >= 0) & (down <= 1) & (across >= 0) & (across <= 1)
    return hit.astype(jnp.bfloat16).reshape(fine.shape[0], -1)


def conv_transpose_folded(weighted, weight):
    rows, frames, cells = weighted.shape
    low = frames // 2
    pooled = jnp.einsum(
        "ots,sq->otq", weighted, pooling(H1, W1), preferred_element_type=jnp.float32
    ).reshape(rows, low, 2, 9, cells // 4)
    even = pooled[:, :, 0] + pooled[:, :, 1]
    after = next_frames(even[:, :1].astype(jnp.bfloat16))
    first = next_frames(pooled[:, :1, 0].astype(jnp.bfloat16)).astype(jnp.float32)
    odd = pooled[:, :, 1] + jnp.concatenate([pooled[:, 1:, 0], first], axis=1)
    even = even.astype(jnp.bfloat16)
    odd = odd.astype(jnp.bfloat16)
    stacked = jnp.stack([jnp.concatenate([even[:, 1:], after], axis=1), odd, even], axis=0)
    return jnp.einsum(
        "dotks,dkco->cts",
        stacked,
        weight.reshape(3, 9, weight.shape[1], rows),
        preferred_element_type=jnp.float32,
    )


def chan_scatter(partial, half):
    me = lax.axis_index("chan")
    mine = lax.dynamic_slice_in_dim(partial, me * half, half, 0)
    other = lax.dynamic_slice_in_dim(partial, (1 - me) * half, half, 0)
    got = lax.ppermute(other.astype(jnp.bfloat16), "chan", [(0, 1), (1, 0)])
    return mine + got.astype(jnp.float32)


def group_norm(values, groups):
    grouped = values.reshape(groups, -1)
    count = grouped.shape[1] * lax.axis_size("tm")
    total, squares = tm_total((jnp.sum(grouped, axis=1), jnp.sum(grouped * grouped, axis=1)))
    mean = total / count
    centered = grouped - mean[:, None]
    variance = squares / count - mean * mean
    inverse = lax.rsqrt(variance + EPS)
    return ((centered * inverse[:, None]).reshape(values.shape), inverse)


def group_sums(grad_norm, normed, groups):
    grads = grad_norm.reshape(groups, -1)
    norms = normed.reshape(groups, -1)
    return tm_total((jnp.sum(grads, axis=1), jnp.sum(grads * norms, axis=1)))


def silu_slope(pre):
    sig = jax.nn.sigmoid(pre)
    return sig * (1.0 + pre * (1.0 - sig))


def next_frames(values):
    return from_behind(values, "tm", -1)


def body(
    features,
    gain_one,
    shift_one,
    conv_one,
    bias_one,
    gain_two,
    shift_two,
    conv_two,
    cotangent,
    frame_weight,
):
    half_in, frames, cells = features.shape
    channels = gain_one.shape[0]
    per_group = channels // GROUPS
    my_groups = half_in // per_group
    offset = lax.axis_index("chan") * half_in
    whole = lax.all_gather(features, "chan", axis=0, tiled=True)
    norm1, inv1 = group_norm(whole.astype(jnp.float32), GROUPS)
    pre1 = norm1 * gain_one[:, None, None] + shift_one[:, None, None]
    act1 = jax.nn.silu(pre1).astype(jnp.bfloat16)
    before = from_behind(act1[:, frames - 2 :], "tm", 1)
    hidden = conv_forward(jnp.concatenate([before, act1], axis=1), conv_one, H1, W1)
    hidden = (hidden + bias_one[:, None, None]).astype(jnp.bfloat16)
    gain_mine = lax.dynamic_slice_in_dim(gain_two, offset, half_in, 0)
    shift_mine = lax.dynamic_slice_in_dim(shift_two, offset, half_in, 0)
    norm2, inv2 = group_norm(hidden.astype(jnp.float32), my_groups)
    pre2 = norm2 * gain_mine[:, None, None] + shift_mine[:, None, None]
    slope2 = silu_slope(pre2) * gain_mine[:, None, None]
    scale = frame_weight.astype(jnp.float32) / 4.0
    weighted = (cotangent.astype(jnp.float32) * scale[None, :, None]).astype(jnp.bfloat16)
    block_sum = chan_scatter(conv_transpose_folded(weighted, conv_two), half_in)
    grad_low = block_sum * slope2
    total_one, total_two = group_sums(grad_low, norm2, my_groups)
    count_hi = 8 * per_group * frames * cells * lax.axis_size("tm")
    first = 8.0 * total_one / count_hi
    second = 8.0 * total_two / count_hi
    grouped = (
        grad_low.reshape(my_groups, -1)
        - first[:, None]
        - norm2.reshape(my_groups, -1) * second[:, None]
    )
    grad_hidden = (grouped * inv2[:, None]).reshape(half_in, frames, cells).astype(jnp.bfloat16)
    hid_ext = jnp.concatenate([grad_hidden, next_frames(grad_hidden[:, :2])], axis=1)
    grad_act1 = chan_scatter(conv_transpose(hid_ext, conv_one, H1, W1), half_in)
    norm_mine = lax.dynamic_slice_in_dim(norm1, offset, half_in, 0)
    pre_mine = lax.dynamic_slice_in_dim(pre1, offset, half_in, 0)
    gain_first = lax.dynamic_slice_in_dim(gain_one, offset, half_in, 0)
    inv_mine = lax.dynamic_slice_in_dim(inv1, offset // per_group, my_groups, 0)
    grad_norm1 = grad_act1 * silu_slope(pre_mine) * gain_first[:, None, None]
    sum_one, sum_two = group_sums(grad_norm1, norm_mine, my_groups)
    count_lo = per_group * frames * cells * lax.axis_size("tm")
    result = (
        grad_norm1.reshape(my_groups, -1)
        - (sum_one / count_lo)[:, None]
        - norm_mine.reshape(my_groups, -1) * (sum_two / count_lo)[:, None]
    )
    return (result * inv_mine[:, None]).reshape(half_in, frames, cells).astype(jnp.bfloat16)


def solution(mesh):
    placed = (
        P("chan", "tm", None),
        P(),
        P(),
        P(None, None, "chan"),
        P("chan"),
        P(),
        P(),
        P(None, None, "chan"),
        P("chan", "tm", None),
        P("tm"),
    )
    return jax.shard_map(
        body, mesh=mesh, in_specs=placed, out_specs=P("chan", "tm", None), check_vma=False
    )
```

```python
import functools

import jax
import jax.numpy as jnp
import numpy as np
from jax import lax
from jax.experimental import pallas as pl
from jax.experimental.pallas import tpu as pltpu
from jax.sharding import PartitionSpec as P

GROUPS = 32
H1 = 8
W1 = 16
CELLS = H1 * W1
EPS = 1e-06
MESH = pl.DeviceIdType.MESH
F32 = jnp.float32
BF16 = jnp.bfloat16
NT = (((1,), (1,)), ((), ()))


def pooling():
    row = np.arange(3 * (2 * H1 + 1) * W1)
    kx, q = row // ((2 * H1 + 1) * W1), row % ((2 * H1 + 1) * W1)
    odd = q >= CELLS
    y0 = np.where(odd, 2 * (q // W1 - H1) - 1, 2 * (q // W1))
    x0 = 2 * (q % W1) + 1 - kx
    fine = np.arange(4 * CELLS)
    down = fine[None] // (2 * W1) - y0[:, None]
    across = fine[None] % (2 * W1) - x0[:, None]
    hit = (down >= 0) & (down <= 1) & (across >= 0) & (across <= 1)
    return jnp.asarray(hit.astype(np.float32), dtype=BF16)


def sigmoid(values):
    return 1.0 / (1.0 + jnp.exp(-values))


def kernel(
    n, frames,
    x_ref, wt_ref, pool_ref, g1_ref, s1_ref, b1_ref, g2_ref, s2_ref, w1_hbm, w2_hbm,
    out_ref,
    w1, w2, fo, hm, ho, wh, even, odd, p2_send, p2_recv, act, hid, low, grad, gh, p1_send, p1_recv,
    acc, stat, slots, tot1, part1,
    load_sem, send_sem, recv_sem, st_send, st_recv,
):
    me = lax.axis_index("tm")
    ch = lax.axis_index("chan")
    oc = 1 - ch
    rows = frames * CELLS
    half = x_ref.shape[1]
    blocks = half // 128
    per_group = 2 * half // GROUPS
    after, before = lax.rem(me + 1, n), lax.rem(me + n - 1, n)
    mine = pl.ds(pl.multiple_of(ch * half, half), half)
    other = pl.ds(pl.multiple_of(oc * half, half), half)

    load2 = pltpu.make_async_copy(w2_hbm, w2, load_sem.at[0])
    load1 = pltpu.make_async_copy(w1_hbm, w1, load_sem.at[1])
    load2.start()
    load1.start()

    barrier = pltpu.get_barrier_semaphore()
    for k in range(1, n):
        pl.semaphore_signal(
            barrier, inc=1, device_id={"tm": lax.rem(me + k, n)}, device_id_type=MESH
        )
    pl.semaphore_signal(barrier, inc=1, device_id={"chan": oc}, device_id_type=MESH)
    pl.semaphore_signal(barrier, inc=1, device_id={"tm": before, "chan": oc}, device_id_type=MESH)
    pl.semaphore_wait(barrier, n + 1)

    def send(index, src, dst, device):
        return pltpu.make_async_remote_copy(
            src_ref=src, dst_ref=dst, send_sem=send_sem.at[index], recv_sem=recv_sem.at[index],
            device_id=device, device_id_type=MESH,
        )

    def sums(index):
        return [
            pltpu.make_async_remote_copy(
                src_ref=stat.at[index], dst_ref=slots.at[index, k],
                send_sem=st_send.at[index, k], recv_sem=st_recv.at[index, k],
                device_id={"tm": lax.rem(me + k, n)}, device_id_type=MESH,
            )
            for k in range(1, n)
        ]

    def start_sums(index, first, second):
        pieces = [v[:, 128 * i : 128 * i + 128] for v in (first, second) for i in range(blocks)]
        pieces.append(jnp.zeros((8 - len(pieces), 128), F32))
        stat[index] = jnp.concatenate(pieces, axis=0)
        copies = sums(index)
        for copy in copies:
            copy.start()
        return copies

    def finish_sums(index, copies):
        for copy in copies:
            copy.wait()
        total = stat[index]
        for k in range(1, n):
            total = total + slots[index, k]
        return total

    in_group = (
        lax.broadcasted_iota(jnp.int32, (half, half), 0) // per_group
        == lax.broadcasted_iota(jnp.int32, (half, half), 1) // per_group
    ).astype(F32)
    count = per_group * rows * n

    def group_means(total):
        first = jnp.concatenate([total[i : i + 1] for i in range(blocks)], axis=1)
        second = jnp.concatenate([total[blocks + i : blocks + i + 1] for i in range(blocks)], axis=1)
        both = jnp.concatenate([first, second, jnp.zeros((6, half), F32)], axis=0)
        spread = jnp.dot(
            both, in_group, precision=lax.Precision.HIGHEST, preferred_element_type=F32
        ) / count
        return spread[0:1], spread[1:2]

    def norm_of(total):
        mean, square = group_means(total)
        return mean, lax.rsqrt(square - mean * mean + EPS)

    def frame(ref, t):
        return ref[t * CELLS : (t + 1) * CELLS, :]

    features = send(0, x_ref, fo, {"chan": oc})
    tail = x_ref.at[pl.ds(rows - 2 * CELLS, 2 * CELLS)]
    halo_mine = send(1, tail, hm, {"tm": after})
    halo_other = send(2, tail, ho, {"tm": after, "chan": oc})
    halo_cot = send(3, wt_ref.at[pl.ds(0, 2)], wh, {"tm": before})
    features.start()
    halo_cot.start()
    halo_mine.start()
    halo_other.start()

    first = jnp.zeros((1, half), F32)
    second = jnp.zeros((1, half), F32)
    for t in range(frames):
        values = frame(x_ref, t).astype(F32)
        first = first + jnp.sum(values, axis=0, keepdims=True)
        second = second + jnp.sum(values * values, axis=0, keepdims=True)
    copies1 = start_sums(0, first, second)

    span = (2 * H1 + 1) * W1
    lanes = wt_ref.shape[2]

    def pooled(values):
        return jnp.dot(pool_ref[...], values, preferred_element_type=F32)

    def keep(ref, t, values):
        for kx in range(3):
            ref[t, :, kx * lanes : (kx + 1) * lanes] = values[kx * span : (kx + 1) * span].astype(BF16)

    def pair(t, _):
        one = pooled(wt_ref[2 * t])
        two = pooled(wt_ref[2 * t + 1])
        keep(even, t, one + two)
        return 0

    lax.fori_loop(0, frames, pair, 0)

    def pair_odd(t, _):
        keep(odd, t, pooled(wt_ref[2 * t + 1]) + pooled(wt_ref[2 * t + 2]))
        return 0

    lax.fori_loop(0, frames - 1, pair_odd, 0)
    halo_cot.wait()
    more = jnp.where(me < n - 1, 1.0, 0.0)
    one = pooled(wh[0]) * more
    two = pooled(wh[1]) * more
    keep(even, frames, one + two)
    keep(odd, frames - 1, pooled(wt_ref[2 * frames - 1]) + one)

    tot1[...] = finish_sums(0, copies1)
    partner = send(4, tot1, part1, {"chan": oc})
    partner.start()

    def conv_two(which):
        acc[...] = jnp.zeros_like(acc)
        for kt in range(3):
            source, t0 = ((even, 1), (odd, 0), (even, 0))[kt]
            for ky in range(3):
                start = (CELLS + W1, 0, CELLS)[ky]
                left = source[t0 : t0 + frames, start : start + CELLS, :].reshape(rows, 3 * lanes)
                tap = 9 * kt + 3 * ky
                right = jnp.concatenate([w2[tap + kx, which, :] for kx in range(3)], axis=1)
                acc[...] += lax.dot_general(left, right, NT, preferred_element_type=F32)

    load2.wait()
    conv_two(other)
    p2_send[...] = acc[...].astype(BF16)
    exchange2 = send(5, p2_send, p2_recv, {"chan": oc})
    exchange2.start()

    cell = lax.broadcasted_iota(jnp.int32, (CELLS, CELLS), 0)
    source = lax.broadcasted_iota(jnp.int32, (CELLS, CELLS), 1)
    left_of = ((source == cell - 1) & (cell % W1 > 0)).astype(F32).astype(BF16)
    right_of = ((source == cell + 1) & (cell % W1 < W1 - 1)).astype(F32).astype(BF16)

    def shifted(values):
        return (
            jnp.dot(left_of, values, preferred_element_type=F32).astype(BF16),
            values,
            jnp.dot(right_of, values, preferred_element_type=F32).astype(BF16),
        )

    inside = slice(W1, W1 + CELLS)
    for ref in (act, grad):
        edge = jnp.zeros((frames + 2, W1, ref.shape[2]), BF16)
        ref[:, :W1, :] = edge
        ref[:, W1 + CELLS :, :] = edge

    partner.wait()
    mean1, inv1 = norm_of(tot1[...])
    mean_o, inv_o = norm_of(part1[...])
    gain1, shift1 = g1_ref[:, mine], s1_ref[:, mine]

    def activate(values, mean, inv, which):
        pre = (values.astype(F32) - mean) * inv * g1_ref[:, which] + s1_ref[:, which]
        return pre * sigmoid(pre)

    def place(t, values, index):
        for kx, moved in enumerate(shifted(values)):
            where = pl.ds(pl.multiple_of(kx * 2 * half + index * half, half), half)
            act[t, inside, where] = moved

    for t in range(frames):
        place(t + 2, activate(frame(x_ref, t), mean1, inv1, mine).astype(BF16), ch)
    halo_mine.wait()
    started = jnp.where(me > 0, 1.0, 0.0)
    for t in range(2):
        place(t, (activate(frame(hm, t), mean1, inv1, mine) * started).astype(BF16), ch)
    features.wait()
    for t in range(frames):
        place(t + 2, activate(frame(fo, t), mean_o, inv_o, other).astype(BF16), oc)
    halo_other.wait()
    for t in range(2):
        place(t, (activate(frame(ho, t), mean_o, inv_o, other) * started).astype(BF16), oc)

    load1.wait()
    acc[...] = jnp.zeros_like(acc)

    def forward(kt, _):
        for ky in range(3):
            left = act[pl.ds(kt, frames), ky * W1 : ky * W1 + CELLS, :].reshape(rows, 6 * half)
            right = w1[pl.ds(9 * kt + 3 * ky, 3)].reshape(6 * half, half)
            acc[...] += jnp.dot(left, right, preferred_element_type=F32)
        return 0

    lax.fori_loop(0, 3, forward, 0)
    first = jnp.zeros((1, half), F32)
    second = jnp.zeros((1, half), F32)
    for t in range(frames):
        values = (frame(acc, t) + b1_ref[...]).astype(BF16)
        hid[t * CELLS : (t + 1) * CELLS, :] = values
        values = values.astype(F32)
        first = first + jnp.sum(values, axis=0, keepdims=True)
        second = second + jnp.sum(values * values, axis=0, keepdims=True)
    copies2 = start_sums(1, first, second)
    conv_two(mine)
    exchange2.wait()

    mean2, inv2 = norm_of(finish_sums(1, copies2))
    gain2, shift2 = g2_ref[:, mine], s2_ref[:, mine]

    def slope(pre):
        sig = sigmoid(pre)
        return sig * (1.0 + pre * (1.0 - sig))

    first = jnp.zeros((1, half), F32)
    second = jnp.zeros((1, half), F32)
    for t in range(frames):
        norm = (frame(hid, t).astype(F32) - mean2) * inv2
        block = frame(acc, t) + frame(p2_recv, t).astype(F32)
        values = block * (slope(norm * gain2 + shift2) * gain2)
        low[t * CELLS : (t + 1) * CELLS, :] = values
        first = first + jnp.sum(values, axis=0, keepdims=True)
        second = second + jnp.sum(values * norm, axis=0, keepdims=True)
    copies3 = start_sums(2, first, second)
    m1, m2 = group_means(finish_sums(2, copies3))

    def put(t, values):
        moved = shifted(values)
        for kx in range(3):
            grad[t, inside, kx * half : (kx + 1) * half] = moved[2 - kx]

    def hidden_grad(t):
        norm = (frame(hid, t).astype(F32) - mean2) * inv2
        return ((frame(low, t) - m1 - norm * m2) * inv2).astype(BF16)

    for t in range(2):
        gh[t] = hidden_grad(t)
    halo_grad = send(6, gh.at[pl.ds(0, 2)], gh.at[pl.ds(2, 2)], {"tm": before})
    halo_grad.start()
    for t in range(frames):
        put(t, gh[t] if t < 2 else hidden_grad(t))

    def back(kt, which):
        for ky in range(3):
            y0 = (2 - ky) * W1
            left = grad[pl.ds(2 - kt, frames), y0 : y0 + CELLS, :].reshape(rows, 3 * half)
            tap = 9 * kt + 3 * ky
            right = jnp.concatenate([w1[tap + kx, which, :] for kx in range(3)], axis=1)
            acc[...] += lax.dot_general(left, right, NT, preferred_element_type=F32)

    acc[...] = jnp.zeros_like(acc)
    back(2, other)
    halo_grad.wait()
    for t in range(2):
        put(frames + t, (gh[2 + t].astype(F32) * more).astype(BF16))
    lax.fori_loop(0, 2, lambda kt, _: (back(kt, other), 0)[1], 0)
    p1_send[...] = acc[...].astype(BF16)
    exchange1 = send(7, p1_send, p1_recv, {"chan": oc})
    exchange1.start()
    acc[...] = jnp.zeros_like(acc)
    lax.fori_loop(0, 3, lambda kt, _: (back(kt, mine), 0)[1], 0)
    exchange1.wait()

    first = jnp.zeros((1, half), F32)
    second = jnp.zeros((1, half), F32)
    for t in range(frames):
        norm = (frame(x_ref, t).astype(F32) - mean1) * inv1
        values = frame(acc, t) + frame(p1_recv, t).astype(F32)
        values = values * slope(norm * gain1 + shift1) * gain1
        low[t * CELLS : (t + 1) * CELLS, :] = values
        first = first + jnp.sum(values, axis=0, keepdims=True)
        second = second + jnp.sum(values * norm, axis=0, keepdims=True)
    copies4 = start_sums(3, first, second)
    m1, m2 = group_means(finish_sums(3, copies4))
    for t in range(frames):
        norm = (frame(x_ref, t).astype(F32) - mean1) * inv1
        values = (frame(low, t) - m1 - norm * m2) * inv1
        out_ref[t * CELLS : (t + 1) * CELLS, :] = values.astype(BF16)


def body(
    features, gain_one, shift_one, conv_one, bias_one, gain_two, shift_two, conv_two, cotangent,
    frame_weight,
):
    half, frames, cells = features.shape
    outs = cotangent.shape[0]
    n = lax.axis_size("tm")
    rows = frames * cells
    across = jnp.transpose(features, (1, 2, 0)).reshape(rows, half)
    scale = frame_weight.astype(F32) / 4.0
    weighted = (cotangent.astype(F32) * scale[None, :, None]).astype(BF16)
    weighted = jnp.transpose(weighted, (1, 2, 0))
    pool = pooling()
    span = pool.shape[0] // 3
    vmem = pl.BlockSpec(memory_space=pltpu.VMEM)
    hbm = pl.BlockSpec(memory_space=pl.ANY)
    out = pl.pallas_call(
        functools.partial(kernel, n, frames),
        out_shape=jax.ShapeDtypeStruct((rows, half), BF16),
        in_specs=[vmem] * 8 + [hbm] * 2,
        out_specs=vmem,
        scratch_shapes=[
            pltpu.VMEM(conv_one.shape, BF16),
            pltpu.VMEM(conv_two.shape, BF16),
            pltpu.VMEM((rows, half), BF16),
            pltpu.VMEM((2 * cells, half), BF16),
            pltpu.VMEM((2 * cells, half), BF16),
            pltpu.VMEM((2, 4 * cells, outs), BF16),
            pltpu.VMEM((frames + 1, span, 3 * outs), BF16),
            pltpu.VMEM((frames, span, 3 * outs), BF16),
            pltpu.VMEM((rows, half), BF16),
            pltpu.VMEM((rows, half), BF16),
            pltpu.VMEM((frames + 2, cells + 2 * W1, 6 * half), BF16),
            pltpu.VMEM((rows, half), BF16),
            pltpu.VMEM((rows, half), F32),
            pltpu.VMEM((frames + 2, cells + 2 * W1, 3 * half), BF16),
            pltpu.VMEM((4, cells, half), BF16),
            pltpu.VMEM((rows, half), BF16),
            pltpu.VMEM((rows, half), BF16),
            pltpu.VMEM((rows, half), F32),
            pltpu.VMEM((4, 8, 128), F32),
            pltpu.VMEM((4, n, 8, 128), F32),
            pltpu.VMEM((8, 128), F32),
            pltpu.VMEM((8, 128), F32),
            pltpu.SemaphoreType.DMA((2,)),
            pltpu.SemaphoreType.DMA((8,)),
            pltpu.SemaphoreType.DMA((8,)),
            pltpu.SemaphoreType.DMA((4, n)),
            pltpu.SemaphoreType.DMA((4, n)),
        ],
        compiler_params=pltpu.CompilerParams(
            collective_id=0, has_side_effects=True, vmem_limit_bytes=48 * 1024 * 1024
        ),
    )(
        across, weighted, pool, gain_one[None], shift_one[None], bias_one[None], gain_two[None],
        shift_two[None], conv_one, conv_two,
    )
    return jnp.transpose(out.reshape(frames, cells, half), (2, 0, 1))


def solution(mesh):
    placed = (
        P("chan", "tm", None),
        P(),
        P(),
        P(None, None, "chan"),
        P("chan"),
        P(),
        P(),
        P(None, None, "chan"),
        P("chan", "tm", None),
        P("tm"),
    )
    return jax.shard_map(
        body, mesh=mesh, in_specs=placed, out_specs=P("chan", "tm", None), check_vma=False
    )
```

```python
import functools

import jax
import jax.numpy as jnp
import numpy as np
from jax import lax
from jax.experimental import pallas as pl
from jax.experimental.pallas import tpu as pltpu
from jax.sharding import PartitionSpec as P

GROUPS = 32
H1 = 8
W1 = 16
CELLS = H1 * W1
EPS = 1e-06
MESH = pl.DeviceIdType.MESH
F32 = jnp.float32
BF16 = jnp.bfloat16
NT = (((1,), (1,)), ((), ()))


def pooling():
    row = np.arange(3 * (2 * H1 + 1) * W1)
    kx, q = row // ((2 * H1 + 1) * W1), row % ((2 * H1 + 1) * W1)
    odd = q >= CELLS
    y0 = np.where(odd, 2 * (q // W1 - H1) - 1, 2 * (q // W1))
    x0 = 2 * (q % W1) + 1 - kx
    fine = np.arange(4 * CELLS)
    down = fine[None] // (2 * W1) - y0[:, None]
    across = fine[None] % (2 * W1) - x0[:, None]
    hit = (down >= 0) & (down <= 1) & (across >= 0) & (across <= 1)
    return jnp.asarray(hit.astype(np.float32), dtype=BF16)


def sigmoid(values):
    return 1.0 / (1.0 + jnp.exp(-values))


def kernel(
    n, frames,
    x_ref, fw_ref, g1_ref, s1_ref, b1_ref, g2_ref, s2_ref, cot_hbm, pool_hbm, w1_hbm, w2_hbm,
    out_ref,
    cot, fine, wt, pool, prev, w1, w2, fo, hm, ho, wh, even, odd, p2_send, p2_recv, act, hid, low, grad, gh, p1_send, p1_recv,
    acc, slope_m, slope_o, stat, slots, tot1, part1, tot4, part4,
    load_sem, send_sem, recv_sem, st_send, st_recv,
):
    me = lax.axis_index("tm")
    ch = lax.axis_index("chan")
    oc = 1 - ch
    rows = frames * CELLS
    half = x_ref.shape[1]
    blocks = half // 128
    per_group = 2 * half // GROUPS
    after, before = lax.rem(me + 1, n), lax.rem(me + n - 1, n)
    mine = pl.ds(pl.multiple_of(ch * half, half), half)
    other = pl.ds(pl.multiple_of(oc * half, half), half)

    load2 = pltpu.make_async_copy(w2_hbm, w2, load_sem.at[0])
    load1 = pltpu.make_async_copy(w1_hbm, w1, load_sem.at[1])
    load_cot = pltpu.make_async_copy(cot_hbm, cot, load_sem.at[2])
    load_pool = pltpu.make_async_copy(pool_hbm, pool, load_sem.at[3])
    load_cot.start()
    load_pool.start()
    load2.start()
    load1.start()

    barrier = pltpu.get_barrier_semaphore()
    for k in range(1, n):
        pl.semaphore_signal(
            barrier, inc=1, device_id={"tm": lax.rem(me + k, n)}, device_id_type=MESH
        )
    pl.semaphore_signal(barrier, inc=1, device_id={"chan": oc}, device_id_type=MESH)
    pl.semaphore_signal(barrier, inc=1, device_id={"tm": before, "chan": oc}, device_id_type=MESH)

    def send(index, src, dst, device):
        return pltpu.make_async_remote_copy(
            src_ref=src, dst_ref=dst, send_sem=send_sem.at[index], recv_sem=recv_sem.at[index],
            device_id=device, device_id_type=MESH,
        )

    def sums(index):
        return [
            pltpu.make_async_remote_copy(
                src_ref=stat.at[index], dst_ref=slots.at[index, k],
                send_sem=st_send.at[index, k], recv_sem=st_recv.at[index, k],
                device_id={"tm": lax.rem(me + k, n)}, device_id_type=MESH,
            )
            for k in range(1, n)
        ]

    def start_sums(index, first, second):
        pieces = [v[:, 128 * i : 128 * i + 128] for v in (first, second) for i in range(blocks)]
        pieces.append(jnp.zeros((8 - len(pieces), 128), F32))
        stat[index] = jnp.concatenate(pieces, axis=0)
        copies = sums(index)
        for copy in copies:
            copy.start()
        return copies

    def finish_sums(index, copies):
        for copy in copies:
            copy.wait()
        total = stat[index]
        for k in range(1, n):
            total = total + slots[index, k]
        return total

    in_group = (
        lax.broadcasted_iota(jnp.int32, (half, half), 0) // per_group
        == lax.broadcasted_iota(jnp.int32, (half, half), 1) // per_group
    ).astype(F32).astype(BF16)
    count = per_group * rows * n

    def group_means(total):
        first = jnp.concatenate([total[i : i + 1] for i in range(blocks)], axis=1)
        second = jnp.concatenate([total[blocks + i : blocks + i + 1] for i in range(blocks)], axis=1)
        both = jnp.concatenate([first, second, jnp.zeros((6, half), F32)], axis=0)
        high = both.astype(BF16).astype(F32)
        middle = (both - high).astype(BF16).astype(F32)
        parts = jnp.concatenate([high, middle, both - high - middle, jnp.zeros_like(both)], axis=0)
        spread = jnp.dot(parts.astype(BF16), in_group, preferred_element_type=F32)
        spread = (spread[0:8] + spread[8:16] + spread[16:24]) / count
        return spread[0:1], spread[1:2]

    def norm_of(total):
        mean, square = group_means(total)
        return mean, lax.rsqrt(square - mean * mean + EPS)

    def frame(ref, t):
        return ref[t * CELLS : (t + 1) * CELLS, :]

    features = send(0, x_ref, fo, {"chan": oc})
    tail = x_ref.at[pl.ds(rows - 2 * CELLS, 2 * CELLS)]
    halo_mine = send(1, tail, hm, {"tm": after})
    halo_other = send(2, tail, ho, {"tm": after, "chan": oc})
    halo_cot = send(3, wt.at[pl.ds(0, 2)], wh, {"tm": before})
    first = jnp.zeros((1, half), F32)
    second = jnp.zeros((1, half), F32)
    for t in range(frames):
        values = frame(x_ref, t).astype(F32)
        first = first + jnp.sum(values, axis=0, keepdims=True)
        second = second + jnp.sum(values * values, axis=0, keepdims=True)

    pl.semaphore_wait(barrier, n + 1)
    features.start()
    halo_mine.start()
    copies1 = start_sums(0, first, second)
    halo_other.start()

    span = (2 * H1 + 1) * W1
    fast = 2 * frames
    lanes = wt.shape[1]
    frame_row = lax.broadcasted_iota(jnp.int32, (fast, 1), 0)
    scale = jnp.zeros((fast, 1), F32)
    for t in range(fast):
        scale = jnp.where(frame_row == t, fw_ref[t].astype(F32) / 4.0, scale)
    load_cot.wait()
    chunk = 16 * fast
    for i in range(lanes // 16):
        where = slice(i * chunk, (i + 1) * chunk)
        values = cot[where, :].astype(F32).reshape(16, fast, 4 * CELLS) * scale[None]
        values = values.reshape(chunk, 4 * CELLS)
        for j in range(4 * CELLS // 128):
            fine[j, where, :] = values[:, 128 * j : 128 * j + 128]
    for t in range(fast):
        for j in range(4 * CELLS // 128):
            values = fine[j, pl.ds(t, lanes, stride=fast), :]
            wt[t, :, 128 * j : 128 * j + 128] = values.astype(BF16)
        if t == 1:
            halo_cot.start()

    def keep(ref, t, values):
        for kx in range(3):
            ref[t, :, kx * lanes : (kx + 1) * lanes] = values[kx * span : (kx + 1) * span].astype(BF16)

    def pooled(values):
        both = lax.dot_general(
            pool[...], values.reshape(2 * lanes, 4 * CELLS), NT, preferred_element_type=F32
        )
        return both[:, :lanes], both[:, lanes:]

    load_pool.wait()
    for t in range(frames):
        one, two = pooled(wt[2 * t : 2 * t + 2])
        keep(even, t, one + two)
        if t > 0:
            keep(odd, t - 1, prev[...] + one)
        prev[...] = two
    halo_cot.wait()
    more = jnp.where(me < n - 1, 1.0, 0.0)
    one, two = pooled(wh[...])
    keep(even, frames, (one + two) * more)
    keep(odd, frames - 1, prev[...] + one * more)

    tot1[...] = finish_sums(0, copies1)
    partner = send(4, tot1, part1, {"chan": oc})
    partner.start()

    def conv_two(which):
        acc[...] = jnp.zeros_like(acc)
        for kt in range(3):
            source, t0 = ((even, 1), (odd, 0), (even, 0))[kt]
            for ky in range(3):
                start = (CELLS + W1, 0, CELLS)[ky]
                left = source[t0 : t0 + frames, start : start + CELLS, :].reshape(rows, 3 * lanes)
                tap = 9 * kt + 3 * ky
                right = jnp.concatenate([w2[tap + kx, which, :] for kx in range(3)], axis=1)
                acc[...] += lax.dot_general(left, right, NT, preferred_element_type=F32)

    load2.wait()
    conv_two(other)
    p2_send[...] = acc[...].astype(BF16)
    exchange2 = send(5, p2_send, p2_recv, {"chan": oc})
    exchange2.start()

    cell = lax.broadcasted_iota(jnp.int32, (CELLS, CELLS), 0)
    source = lax.broadcasted_iota(jnp.int32, (CELLS, CELLS), 1)
    left_of = ((source == cell - 1) & (cell % W1 > 0)).astype(F32).astype(BF16)
    right_of = ((source == cell + 1) & (cell % W1 < W1 - 1)).astype(F32).astype(BF16)

    def shifted(values):
        return (
            jnp.dot(left_of, values, preferred_element_type=F32).astype(BF16),
            values,
            jnp.dot(right_of, values, preferred_element_type=F32).astype(BF16),
        )

    inside = slice(W1, W1 + CELLS)
    for ref in (act, grad):
        edge = jnp.zeros((frames + 2, W1, ref.shape[2]), BF16)
        ref[:, :W1, :] = edge
        ref[:, W1 + CELLS :, :] = edge

    partner.wait()
    mean1, inv1 = norm_of(tot1[...])
    mean_o, inv_o = norm_of(part1[...])
    gain1, shift1 = g1_ref[:, mine], s1_ref[:, mine]

    def activate(values, mean, inv, which):
        pre = (values.astype(F32) - mean) * inv * g1_ref[:, which] + s1_ref[:, which]
        return pre * sigmoid(pre)

    def place(t, values, index):
        for kx, moved in enumerate(shifted(values)):
            where = pl.ds(pl.multiple_of(kx * 2 * half + index * half, half), half)
            act[t, inside, where] = moved

    for t in range(frames):
        place(t + 2, activate(frame(x_ref, t), mean1, inv1, mine).astype(BF16), ch)
    halo_mine.wait()
    started = jnp.where(me > 0, 1.0, 0.0)
    for t in range(2):
        place(t, (activate(frame(hm, t), mean1, inv1, mine) * started).astype(BF16), ch)
    features.wait()
    for t in range(frames):
        place(t + 2, activate(frame(fo, t), mean_o, inv_o, other).astype(BF16), oc)
    halo_other.wait()
    for t in range(2):
        place(t, (activate(frame(ho, t), mean_o, inv_o, other) * started).astype(BF16), oc)

    load1.wait()
    acc[...] = jnp.zeros_like(acc)

    def forward(kt, _):
        for ky in range(3):
            left = act[pl.ds(kt, frames), ky * W1 : ky * W1 + CELLS, :].reshape(rows, 6 * half)
            right = w1[pl.ds(9 * kt + 3 * ky, 3)].reshape(6 * half, half)
            acc[...] += jnp.dot(left, right, preferred_element_type=F32)
        return 0

    lax.fori_loop(0, 3, forward, 0)
    first = jnp.zeros((1, half), F32)
    second = jnp.zeros((1, half), F32)
    for t in range(frames):
        values = (frame(acc, t) + b1_ref[...]).astype(BF16)
        hid[t * CELLS : (t + 1) * CELLS, :] = values
        values = values.astype(F32)
        first = first + jnp.sum(values, axis=0, keepdims=True)
        second = second + jnp.sum(values * values, axis=0, keepdims=True)
    copies2 = start_sums(1, first, second)
    conv_two(mine)
    exchange2.wait()

    mean2, inv2 = norm_of(finish_sums(1, copies2))
    gain2, shift2 = g2_ref[:, mine], s2_ref[:, mine]

    def slope(pre):
        sig = sigmoid(pre)
        return sig * (1.0 + pre * (1.0 - sig))

    first = jnp.zeros((1, half), F32)
    second = jnp.zeros((1, half), F32)
    for t in range(frames):
        norm = (frame(hid, t).astype(F32) - mean2) * inv2
        block = frame(acc, t) + frame(p2_recv, t).astype(F32)
        values = block * (slope(norm * gain2 + shift2) * gain2)
        low[t * CELLS : (t + 1) * CELLS, :] = values
        first = first + jnp.sum(values, axis=0, keepdims=True)
        second = second + jnp.sum(values * norm, axis=0, keepdims=True)
    copies3 = start_sums(2, first, second)

    def norm_one(t):
        return (frame(x_ref, t).astype(F32) - mean1) * inv1

    def norm_other(t):
        return (frame(fo, t).astype(F32) - mean_o) * inv_o

    gain_o, shift_o = g1_ref[:, other], s1_ref[:, other]
    for t in range(frames):
        part = slice(t * CELLS, (t + 1) * CELLS)
        slope_m[part, :] = slope(norm_one(t) * gain1 + shift1) * gain1
        slope_o[part, :] = slope(norm_other(t) * gain_o + shift_o) * gain_o
    m1, m2 = group_means(finish_sums(2, copies3))

    def put(t, values):
        moved = shifted(values)
        for kx in range(3):
            grad[t, inside, kx * half : (kx + 1) * half] = moved[2 - kx]

    def hidden_grad(t):
        norm = (frame(hid, t).astype(F32) - mean2) * inv2
        return ((frame(low, t) - m1 - norm * m2) * inv2).astype(BF16)

    for t in range(2):
        gh[t] = hidden_grad(t)
    halo_grad = send(6, gh.at[pl.ds(0, 2)], gh.at[pl.ds(2, 2)], {"tm": before})
    halo_grad.start()
    for t in range(frames):
        put(t, gh[t] if t < 2 else hidden_grad(t))

    def back(kt, which):
        for ky in range(3):
            y0 = (2 - ky) * W1
            left = grad[pl.ds(2 - kt, frames), y0 : y0 + CELLS, :].reshape(rows, 3 * half)
            tap = 9 * kt + 3 * ky
            right = jnp.concatenate([w1[tap + kx, which, :] for kx in range(3)], axis=1)
            acc[...] += lax.dot_general(left, right, NT, preferred_element_type=F32)

    acc[...] = jnp.zeros_like(acc)
    back(2, other)
    halo_grad.wait()
    for t in range(2):
        put(frames + t, (gh[2 + t].astype(F32) * more).astype(BF16))
    lax.fori_loop(0, 2, lambda kt, _: (back(kt, other), 0)[1], 0)
    p1_send[...] = acc[...].astype(BF16)
    exchange1 = send(7, p1_send, p1_recv, {"chan": oc})
    exchange1.start()

    def slope_sums(slopes, norm_at):
        first = jnp.zeros((1, half), F32)
        second = jnp.zeros((1, half), F32)
        for t in range(frames):
            values = frame(acc, t) * frame(slopes, t)
            first = first + jnp.sum(values, axis=0, keepdims=True)
            second = second + jnp.sum(values * norm_at(t), axis=0, keepdims=True)
        return first, second

    copies4 = start_sums(3, *slope_sums(slope_o, norm_other))
    acc[...] = jnp.zeros_like(acc)
    lax.fori_loop(0, 3, lambda kt, _: (back(kt, mine), 0)[1], 0)
    copies5 = start_sums(4, *slope_sums(slope_m, norm_one))
    tot4[...] = finish_sums(3, copies4)
    partner4 = send(8, tot4, part4, {"chan": oc})
    partner4.start()
    total = finish_sums(4, copies5)
    partner4.wait()
    m1, m2 = group_means(total + part4[...])
    exchange1.wait()
    for t in range(frames):
        values = (frame(acc, t) + frame(p1_recv, t).astype(F32)) * frame(slope_m, t)
        values = (values - m1 - norm_one(t) * m2) * inv1
        out_ref[t * CELLS : (t + 1) * CELLS, :] = values.astype(BF16)


def body(
    features, gain_one, shift_one, conv_one, bias_one, gain_two, shift_two, conv_two, cotangent,
    frame_weight,
):
    half, frames, cells = features.shape
    outs = cotangent.shape[0]
    n = lax.axis_size("tm")
    rows = frames * cells
    across = jnp.transpose(features, (1, 2, 0)).reshape(rows, half)
    fine = cotangent.reshape(outs * cotangent.shape[1], cotangent.shape[2])
    pool = pooling()
    span = pool.shape[0] // 3
    vmem = pl.BlockSpec(memory_space=pltpu.VMEM)
    hbm = pl.BlockSpec(memory_space=pl.ANY)
    out = pl.pallas_call(
        functools.partial(kernel, n, frames),
        out_shape=jax.ShapeDtypeStruct((rows, half), BF16),
        in_specs=[vmem, pl.BlockSpec(memory_space=pltpu.SMEM)] + [vmem] * 5 + [hbm] * 4,
        out_specs=vmem,
        scratch_shapes=[
            pltpu.VMEM(fine.shape, BF16),
            pltpu.VMEM((4 * cells // 128, fine.shape[0], 128), F32),
            pltpu.VMEM((2 * frames, outs, 4 * cells), BF16),
            pltpu.VMEM(pool.shape, BF16),
            pltpu.VMEM((pool.shape[0], outs), F32),
            pltpu.VMEM(conv_one.shape, BF16),
            pltpu.VMEM(conv_two.shape, BF16),
            pltpu.VMEM((rows, half), BF16),
            pltpu.VMEM((2 * cells, half), BF16),
            pltpu.VMEM((2 * cells, half), BF16),
            pltpu.VMEM((2, outs, 4 * cells), BF16),
            pltpu.VMEM((frames + 1, span, 3 * outs), BF16),
            pltpu.VMEM((frames, span, 3 * outs), BF16),
            pltpu.VMEM((rows, half), BF16),
            pltpu.VMEM((rows, half), BF16),
            pltpu.VMEM((frames + 2, cells + 2 * W1, 6 * half), BF16),
            pltpu.VMEM((rows, half), BF16),
            pltpu.VMEM((rows, half), F32),
            pltpu.VMEM((frames + 2, cells + 2 * W1, 3 * half), BF16),
            pltpu.VMEM((4, cells, half), BF16),
            pltpu.VMEM((rows, half), BF16),
            pltpu.VMEM((rows, half), BF16),
            pltpu.VMEM((rows, half), F32),
            pltpu.VMEM((rows, half), F32),
            pltpu.VMEM((rows, half), F32),
            pltpu.VMEM((5, 8, 128), F32),
            pltpu.VMEM((5, n, 8, 128), F32),
            pltpu.VMEM((8, 128), F32),
            pltpu.VMEM((8, 128), F32),
            pltpu.VMEM((8, 128), F32),
            pltpu.VMEM((8, 128), F32),
            pltpu.SemaphoreType.DMA((4,)),
            pltpu.SemaphoreType.DMA((9,)),
            pltpu.SemaphoreType.DMA((9,)),
            pltpu.SemaphoreType.DMA((5, n)),
            pltpu.SemaphoreType.DMA((5, n)),
        ],
        compiler_params=pltpu.CompilerParams(
            collective_id=0, has_side_effects=True, vmem_limit_bytes=56 * 1024 * 1024
        ),
    )(
        across, frame_weight, gain_one[None], shift_one[None], bias_one[None], gain_two[None],
        shift_two[None], fine, pool, conv_one, conv_two,
    )
    return jnp.transpose(out.reshape(frames, cells, half), (2, 0, 1))


def solution(mesh):
    placed = (
        P("chan", "tm", None),
        P(),
        P(),
        P(None, None, "chan"),
        P("chan"),
        P(),
        P(),
        P(None, None, "chan"),
        P("chan", "tm", None),
        P("tm"),
    )
    return jax.shard_map(
        body, mesh=mesh, in_specs=placed, out_specs=P("chan", "tm", None), check_vma=False
    )
```

```python
import functools

import jax
import jax.numpy as jnp
import numpy as np
from jax import lax
from jax.experimental import pallas as pl
from jax.experimental.pallas import tpu as pltpu
from jax.sharding import PartitionSpec as P

GROUPS = 32
H1 = 8
W1 = 16
CELLS = H1 * W1
EPS = 1e-06
MESH = pl.DeviceIdType.MESH
F32 = jnp.float32
BF16 = jnp.bfloat16
NT = (((1,), (1,)), ((), ()))


def pooling():
    row = np.arange(3 * (2 * H1 + 1) * W1)
    kx, q = row // ((2 * H1 + 1) * W1), row % ((2 * H1 + 1) * W1)
    odd = q >= CELLS
    y0 = np.where(odd, 2 * (q // W1 - H1) - 1, 2 * (q // W1))
    x0 = 2 * (q % W1) + 1 - kx
    fine = np.arange(4 * CELLS)
    down = fine[None] // (2 * W1) - y0[:, None]
    across = fine[None] % (2 * W1) - x0[:, None]
    hit = (down >= 0) & (down <= 1) & (across >= 0) & (across <= 1)
    return jnp.asarray(hit.astype(np.float32), dtype=BF16)


def sigmoid(values):
    return 1.0 / (1.0 + jnp.exp(-values))


def kernel(
    n, frames,
    x_ref, fw_ref, g1_ref, s1_ref, b1_ref, g2_ref, s2_ref, cot_hbm, pool_hbm, w1_hbm, w2_hbm,
    out_ref,
    cot, fine, wt, pool, prev, w1, w2, fo, hm, ho, wh, even, odd, p2_send, p2_recv, act_m, act_o, hid, low, grad, gh, p1_send, p1_recv,
    acc, slope_m, slope_o, stat, slots, tot1, part1, tot4, part4,
    load_sem, send_sem, recv_sem, st_send, st_recv,
):
    me = lax.axis_index("tm")
    ch = lax.axis_index("chan")
    oc = 1 - ch
    rows = frames * CELLS
    half = x_ref.shape[1]
    blocks = half // 128
    per_group = 2 * half // GROUPS
    after, before = lax.rem(me + 1, n), lax.rem(me + n - 1, n)
    mine = pl.ds(pl.multiple_of(ch * half, half), half)
    other = pl.ds(pl.multiple_of(oc * half, half), half)

    load2 = pltpu.make_async_copy(w2_hbm, w2, load_sem.at[0])
    load1 = pltpu.make_async_copy(w1_hbm, w1, load_sem.at[1])
    load_cot = pltpu.make_async_copy(cot_hbm, cot, load_sem.at[2])
    load_pool = pltpu.make_async_copy(pool_hbm, pool, load_sem.at[3])
    load_cot.start()
    load_pool.start()
    load2.start()
    load1.start()

    barrier = pltpu.get_barrier_semaphore()
    for k in range(1, n):
        pl.semaphore_signal(
            barrier, inc=1, device_id={"tm": lax.rem(me + k, n)}, device_id_type=MESH
        )
    pl.semaphore_signal(barrier, inc=1, device_id={"chan": oc}, device_id_type=MESH)

    def send(index, src, dst, device):
        return pltpu.make_async_remote_copy(
            src_ref=src, dst_ref=dst, send_sem=send_sem.at[index], recv_sem=recv_sem.at[index],
            device_id=device, device_id_type=MESH,
        )

    def sums(index):
        return [
            pltpu.make_async_remote_copy(
                src_ref=stat.at[index], dst_ref=slots.at[index, k],
                send_sem=st_send.at[index], recv_sem=st_recv.at[index],
                device_id={"tm": lax.rem(me + k, n)}, device_id_type=MESH,
            )
            for k in range(1, n)
        ]

    def all_sums(index):
        block = slots.at[index, pl.ds(1, n - 1)]
        return pltpu.make_async_remote_copy(
            src_ref=block, dst_ref=block, send_sem=st_send.at[index], recv_sem=st_recv.at[index],
            device_id={"tm": after}, device_id_type=MESH,
        )

    def start_sums(index, first, second):
        pieces = [v[:, 128 * i : 128 * i + 128] for v in (first, second) for i in range(blocks)]
        pieces.append(jnp.zeros((8 - len(pieces), 128), F32))
        stat[index] = jnp.concatenate(pieces, axis=0)
        for copy in sums(index):
            copy.start()

    def finish_sums(index):
        all_sums(index).wait_recv()
        total = stat[index]
        for k in range(1, n):
            total = total + slots[index, k]
        return total

    in_group = (
        lax.broadcasted_iota(jnp.int32, (half, half), 0) // per_group
        == lax.broadcasted_iota(jnp.int32, (half, half), 1) // per_group
    ).astype(F32).astype(BF16)
    count = per_group * rows * n

    def group_means(total):
        first = jnp.concatenate([total[i : i + 1] for i in range(blocks)], axis=1)
        second = jnp.concatenate([total[blocks + i : blocks + i + 1] for i in range(blocks)], axis=1)
        both = jnp.concatenate([first, second, jnp.zeros((6, half), F32)], axis=0)
        high = both.astype(BF16).astype(F32)
        middle = (both - high).astype(BF16).astype(F32)
        parts = jnp.concatenate([high, middle, both - high - middle, jnp.zeros_like(both)], axis=0)
        spread = jnp.dot(parts.astype(BF16), in_group, preferred_element_type=F32)
        spread = (spread[0:8] + spread[8:16] + spread[16:24]) / count
        return spread[0:1], spread[1:2]

    def norm_of(total):
        mean, square = group_means(total)
        return mean, lax.rsqrt(square - mean * mean + EPS)

    def frame(ref, t):
        return ref[t * CELLS : (t + 1) * CELLS, :]

    early, late = pl.ds(0, rows - 2 * CELLS), pl.ds(rows - 2 * CELLS, 2 * CELLS)
    tail = x_ref.at[late]
    features_late = send(9, tail, fo.at[late], {"chan": oc})
    features = send(0, x_ref.at[early], fo.at[early], {"chan": oc})
    halo_mine = send(1, tail, hm, {"tm": after})
    halo_other = send(2, fo.at[late], ho, {"tm": after})
    halo_cot = send(3, wt.at[pl.ds(0, 2)], wh, {"tm": before})
    first = jnp.zeros((1, half), F32)
    second = jnp.zeros((1, half), F32)
    for t in range(frames):
        values = frame(x_ref, t).astype(F32)
        first = first + jnp.sum(values, axis=0, keepdims=True)
        second = second + jnp.sum(values * values, axis=0, keepdims=True)

    pl.semaphore_wait(barrier, n)
    features_late.start()
    start_sums(0, first, second)
    halo_mine.start()
    features.start()

    span = (2 * H1 + 1) * W1
    fast = 2 * frames
    lanes = wt.shape[1]
    frame_row = lax.broadcasted_iota(jnp.int32, (fast, 1), 0)
    scale = jnp.zeros((fast, 1), F32)
    for t in range(fast):
        scale = jnp.where(frame_row == t, fw_ref[t].astype(F32) / 4.0, scale)
    load_cot.wait()
    chunk = 16 * fast
    for i in range(lanes // 16):
        where = slice(i * chunk, (i + 1) * chunk)
        values = cot[where, :].astype(F32).reshape(16, fast, 4 * CELLS) * scale[None]
        values = values.reshape(chunk, 4 * CELLS)
        for j in range(4 * CELLS // 128):
            fine[j, where, :] = values[:, 128 * j : 128 * j + 128]
    for t in range(fast):
        for j in range(4 * CELLS // 128):
            values = fine[j, pl.ds(t, lanes, stride=fast), :]
            wt[t, :, 128 * j : 128 * j + 128] = values.astype(BF16)
        if t == 1:
            halo_cot.start()

    def keep(ref, t, values):
        for kx in range(3):
            ref[t, :, kx * lanes : (kx + 1) * lanes] = values[kx * span : (kx + 1) * span].astype(BF16)

    def pooled(values):
        both = lax.dot_general(
            pool[...], values.reshape(2 * lanes, 4 * CELLS), NT, preferred_element_type=F32
        )
        return both[:, :lanes], both[:, lanes:]

    features_late.wait()
    halo_other.start()
    load_pool.wait()
    for t in range(frames):
        one, two = pooled(wt[2 * t : 2 * t + 2])
        keep(even, t, one + two)
        if t > 0:
            keep(odd, t - 1, prev[...] + one)
        prev[...] = two
    halo_cot.wait()
    more = jnp.where(me < n - 1, 1.0, 0.0)
    one, two = pooled(wh[...])
    keep(even, frames, (one + two) * more)
    keep(odd, frames - 1, prev[...] + one * more)

    tot1[...] = finish_sums(0)
    partner = send(4, tot1, part1, {"chan": oc})
    partner.start()

    cell = lax.broadcasted_iota(jnp.int32, (CELLS, CELLS), 0)
    source = lax.broadcasted_iota(jnp.int32, (CELLS, CELLS), 1)
    left_of = ((source == cell - 1) & (cell % W1 > 0)).astype(F32).astype(BF16)
    right_of = ((source == cell + 1) & (cell % W1 < W1 - 1)).astype(F32).astype(BF16)

    def shifted(values):
        return (
            jnp.dot(left_of, values, preferred_element_type=F32).astype(BF16),
            values,
            jnp.dot(right_of, values, preferred_element_type=F32).astype(BF16),
        )

    inside = slice(W1, W1 + CELLS)
    for ref in (act_m, act_o, grad):
        edge = jnp.zeros((frames + 2, W1, ref.shape[2]), BF16)
        ref[:, :W1, :] = edge
        ref[:, W1 + CELLS :, :] = edge

    def activate(values, mean, inv, which):
        pre = (values.astype(F32) - mean) * inv * g1_ref[:, which] + s1_ref[:, which]
        return pre * sigmoid(pre)

    def place(ref, t, values):
        for kx, moved in enumerate(shifted(values.astype(BF16))):
            ref[t, inside, kx * half : (kx + 1) * half] = moved

    def forward(ref, which):
        for kt in range(3):
            for ky in range(3):
                left = ref[kt : kt + frames, ky * W1 : ky * W1 + CELLS, :].reshape(rows, 3 * half)
                tap = 9 * kt + 3 * ky
                right = jnp.concatenate([w1[tap + kx, which, :] for kx in range(3)], axis=0)
                acc[...] += jnp.dot(left, right, preferred_element_type=F32)

    started = jnp.where(me > 0, 1.0, 0.0)
    mean1, inv1 = norm_of(tot1[...])
    gain1, shift1 = g1_ref[:, mine], s1_ref[:, mine]
    acc[...] = jnp.zeros_like(acc)
    for t in range(frames):
        place(act_m, t + 2, activate(frame(x_ref, t), mean1, inv1, mine))
    halo_mine.wait()
    for t in range(2):
        place(act_m, t, activate(frame(hm, t), mean1, inv1, mine) * started)
    load1.wait()
    forward(act_m, mine)

    def conv_two(which):
        low[...] = jnp.zeros_like(low)
        for kt in range(3):
            source, t0 = ((even, 1), (odd, 0), (even, 0))[kt]
            for ky in range(3):
                start = (CELLS + W1, 0, CELLS)[ky]
                left = source[t0 : t0 + frames, start : start + CELLS, :].reshape(rows, 3 * lanes)
                tap = 9 * kt + 3 * ky
                right = jnp.concatenate([w2[tap + kx, which, :] for kx in range(3)], axis=1)
                low[...] += lax.dot_general(left, right, NT, preferred_element_type=F32)

    load2.wait()
    conv_two(other)
    p2_send[...] = low[...].astype(BF16)
    exchange2 = send(5, p2_send, p2_recv, {"chan": oc})
    exchange2.start()

    partner.wait()
    mean_o, inv_o = norm_of(part1[...])
    features.wait()
    for t in range(frames):
        place(act_o, t + 2, activate(frame(fo, t), mean_o, inv_o, other))
    halo_other.wait()
    for t in range(2):
        place(act_o, t, activate(frame(ho, t), mean_o, inv_o, other) * started)
    forward(act_o, other)
    first = jnp.zeros((1, half), F32)
    second = jnp.zeros((1, half), F32)
    for t in range(frames):
        values = (frame(acc, t) + b1_ref[...]).astype(BF16)
        hid[t * CELLS : (t + 1) * CELLS, :] = values
        values = values.astype(F32)
        first = first + jnp.sum(values, axis=0, keepdims=True)
        second = second + jnp.sum(values * values, axis=0, keepdims=True)
    start_sums(1, first, second)
    conv_two(mine)
    exchange2.wait()

    mean2, inv2 = norm_of(finish_sums(1))
    gain2, shift2 = g2_ref[:, mine], s2_ref[:, mine]

    def slope(pre):
        sig = sigmoid(pre)
        return sig * (1.0 + pre * (1.0 - sig))

    first = jnp.zeros((1, half), F32)
    second = jnp.zeros((1, half), F32)
    for t in range(frames):
        norm = (frame(hid, t).astype(F32) - mean2) * inv2
        block = frame(low, t) + frame(p2_recv, t).astype(F32)
        values = block * (slope(norm * gain2 + shift2) * gain2)
        low[t * CELLS : (t + 1) * CELLS, :] = values
        first = first + jnp.sum(values, axis=0, keepdims=True)
        second = second + jnp.sum(values * norm, axis=0, keepdims=True)
    start_sums(2, first, second)

    def norm_one(t):
        return (frame(x_ref, t).astype(F32) - mean1) * inv1

    def norm_other(t):
        return (frame(fo, t).astype(F32) - mean_o) * inv_o

    gain_o, shift_o = g1_ref[:, other], s1_ref[:, other]
    for t in range(frames):
        part = slice(t * CELLS, (t + 1) * CELLS)
        slope_m[part, :] = slope(norm_one(t) * gain1 + shift1) * gain1
        slope_o[part, :] = slope(norm_other(t) * gain_o + shift_o) * gain_o
    m1, m2 = group_means(finish_sums(2))

    def put(t, values):
        moved = shifted(values)
        for kx in range(3):
            grad[t, inside, kx * half : (kx + 1) * half] = moved[2 - kx]

    def hidden_grad(t):
        norm = (frame(hid, t).astype(F32) - mean2) * inv2
        return ((frame(low, t) - m1 - norm * m2) * inv2).astype(BF16)

    for t in range(2):
        gh[t] = hidden_grad(t)
    halo_grad = send(6, gh.at[pl.ds(0, 2)], gh.at[pl.ds(2, 2)], {"tm": before})
    halo_grad.start()
    for t in range(frames):
        put(t, gh[t] if t < 2 else hidden_grad(t))

    def back(t0, count, which):
        part = pl.ds(t0 * CELLS, count * CELLS)
        total = jnp.zeros((count * CELLS, half), F32)
        acc[part, :] = total

        def add(kt, _):
            for ky in range(3):
                y0 = (2 - ky) * W1
                left = grad[pl.ds(t0 + 2 - kt, count), y0 : y0 + CELLS, :]
                tap = 9 * kt + 3 * ky
                right = jnp.concatenate([w1[tap + kx, which, :] for kx in range(3)], axis=1)
                acc[part, :] += lax.dot_general(
                    left.reshape(count * CELLS, 3 * half), right, NT, preferred_element_type=F32
                )
            return 0

        lax.fori_loop(0, 3, add, 0)

    def send_back(index, t0, count):
        part = pl.ds(t0 * CELLS, count * CELLS)
        p1_send[part, :] = acc[part, :].astype(BF16)
        copy = send(index, p1_send.at[part], p1_recv.at[part], {"chan": oc})
        copy.start()
        return copy

    back(0, frames - 2, other)
    exchange1 = [send_back(7, 0, frames - 2)]
    halo_grad.wait()
    for t in range(2):
        put(frames + t, (gh[2 + t].astype(F32) * more).astype(BF16))
    back(frames - 2, 2, other)
    exchange1.append(send_back(2 + 8, frames - 2, 2))

    def slope_sums(slopes, norm_at):
        first = jnp.zeros((1, half), F32)
        second = jnp.zeros((1, half), F32)
        for t in range(frames):
            values = frame(acc, t) * frame(slopes, t)
            first = first + jnp.sum(values, axis=0, keepdims=True)
            second = second + jnp.sum(values * norm_at(t), axis=0, keepdims=True)
        return first, second

    start_sums(3, *slope_sums(slope_o, norm_other))
    back(0, frames, mine)
    start_sums(4, *slope_sums(slope_m, norm_one))
    tot4[...] = finish_sums(3)
    partner4 = send(8, tot4, part4, {"chan": oc})
    partner4.start()
    total = finish_sums(4)
    partner4.wait()
    m1, m2 = group_means(total + part4[...])
    for copy in exchange1:
        copy.wait()
    for t in range(frames):
        values = (frame(acc, t) + frame(p1_recv, t).astype(F32)) * frame(slope_m, t)
        values = (values - m1 - norm_one(t) * m2) * inv1
        out_ref[t * CELLS : (t + 1) * CELLS, :] = values.astype(BF16)
    for index in range(5):
        all_sums(index).wait_send()


def body(
    features, gain_one, shift_one, conv_one, bias_one, gain_two, shift_two, conv_two, cotangent,
    frame_weight,
):
    half, frames, cells = features.shape
    outs = cotangent.shape[0]
    n = lax.axis_size("tm")
    rows = frames * cells
    across = jnp.transpose(features, (1, 2, 0)).reshape(rows, half)
    fine = cotangent.reshape(outs * cotangent.shape[1], cotangent.shape[2])
    pool = pooling()
    span = pool.shape[0] // 3
    vmem = pl.BlockSpec(memory_space=pltpu.VMEM)
    hbm = pl.BlockSpec(memory_space=pl.ANY)
    out = pl.pallas_call(
        functools.partial(kernel, n, frames),
        out_shape=jax.ShapeDtypeStruct((rows, half), BF16),
        in_specs=[vmem, pl.BlockSpec(memory_space=pltpu.SMEM)] + [vmem] * 5 + [hbm] * 4,
        out_specs=vmem,
        scratch_shapes=[
            pltpu.VMEM(fine.shape, BF16),
            pltpu.VMEM((4 * cells // 128, fine.shape[0], 128), F32),
            pltpu.VMEM((2 * frames, outs, 4 * cells), BF16),
            pltpu.VMEM(pool.shape, BF16),
            pltpu.VMEM((pool.shape[0], outs), F32),
            pltpu.VMEM(conv_one.shape, BF16),
            pltpu.VMEM(conv_two.shape, BF16),
            pltpu.VMEM((rows, half), BF16),
            pltpu.VMEM((2 * cells, half), BF16),
            pltpu.VMEM((2 * cells, half), BF16),
            pltpu.VMEM((2, outs, 4 * cells), BF16),
            pltpu.VMEM((frames + 1, span, 3 * outs), BF16),
            pltpu.VMEM((frames, span, 3 * outs), BF16),
            pltpu.VMEM((rows, half), BF16),
            pltpu.VMEM((rows, half), BF16),
            pltpu.VMEM((frames + 2, cells + 2 * W1, 3 * half), BF16),
            pltpu.VMEM((frames + 2, cells + 2 * W1, 3 * half), BF16),
            pltpu.VMEM((rows, half), BF16),
            pltpu.VMEM((rows, half), F32),
            pltpu.VMEM((frames + 2, cells + 2 * W1, 3 * half), BF16),
            pltpu.VMEM((4, cells, half), BF16),
            pltpu.VMEM((rows, half), BF16),
            pltpu.VMEM((rows, half), BF16),
            pltpu.VMEM((rows, half), F32),
            pltpu.VMEM((rows, half), F32),
            pltpu.VMEM((rows, half), F32),
            pltpu.VMEM((5, 8, 128), F32),
            pltpu.VMEM((5, n, 8, 128), F32),
            pltpu.VMEM((8, 128), F32),
            pltpu.VMEM((8, 128), F32),
            pltpu.VMEM((8, 128), F32),
            pltpu.VMEM((8, 128), F32),
            pltpu.SemaphoreType.DMA((4,)),
            pltpu.SemaphoreType.DMA((11,)),
            pltpu.SemaphoreType.DMA((11,)),
            pltpu.SemaphoreType.DMA((5,)),
            pltpu.SemaphoreType.DMA((5,)),
        ],
        compiler_params=pltpu.CompilerParams(
            collective_id=0, has_side_effects=True, vmem_limit_bytes=56 * 1024 * 1024
        ),
    )(
        across, frame_weight, gain_one[None], shift_one[None], bias_one[None], gain_two[None],
        shift_two[None], fine, pool, conv_one, conv_two,
    )
    return jnp.transpose(out.reshape(frames, cells, half), (2, 0, 1))


def solution(mesh):
    placed = (
        P("chan", "tm", None),
        P(),
        P(),
        P(None, None, "chan"),
        P("chan"),
        P(),
        P(),
        P(None, None, "chan"),
        P("chan", "tm", None),
        P("tm"),
    )
    return jax.shard_map(
        body, mesh=mesh, in_specs=placed, out_specs=P("chan", "tm", None), check_vma=False
    )
```

```python
import functools

import jax
import jax.numpy as jnp
import numpy as np
from jax import lax
from jax.experimental import pallas as pl
from jax.experimental.pallas import tpu as pltpu
from jax.sharding import PartitionSpec as P

GROUPS = 32
H1 = 8
W1 = 16
CELLS = H1 * W1
EPS = 1e-06
MESH = pl.DeviceIdType.MESH
F32 = jnp.float32
BF16 = jnp.bfloat16
NT = (((1,), (1,)), ((), ()))


def pooling():
    row = np.arange(3 * (2 * H1 + 1) * W1)
    kx, q = row // ((2 * H1 + 1) * W1), row % ((2 * H1 + 1) * W1)
    odd = q >= CELLS
    y0 = np.where(odd, 2 * (q // W1 - H1) - 1, 2 * (q // W1))
    x0 = 2 * (q % W1) + 1 - kx
    fine = np.arange(4 * CELLS)
    down = fine[None] // (2 * W1) - y0[:, None]
    across = fine[None] % (2 * W1) - x0[:, None]
    hit = (down >= 0) & (down <= 1) & (across >= 0) & (across <= 1)
    return jnp.asarray(hit.astype(np.float32), dtype=BF16)


def sigmoid(values):
    return 1.0 / (1.0 + jnp.exp(-values))


def kernel(
    n, frames,
    x_ref, fw_ref, g1_ref, s1_ref, b1_ref, g2_ref, s2_ref, cot_hbm, pool_hbm, w1_hbm, w2_hbm,
    out_ref,
    cot, fine, wt, pool, prev, w1, w2, fo, hm, ho, wh, even, odd, p2_send, p2_recv, act_m, act_o, hid, low, grad, gh, p1_send, p1_recv,
    acc, slope_m, slope_o, stat, slots, tot1, part1, tot4, part4,
    load_sem, send_sem, recv_sem, st_send, st_recv,
):
    me = lax.axis_index("tm")
    ch = lax.axis_index("chan")
    oc = 1 - ch
    rows = frames * CELLS
    half = x_ref.shape[1]
    blocks = half // 128
    per_group = 2 * half // GROUPS
    after, before = lax.rem(me + 1, n), lax.rem(me + n - 1, n)
    mine = pl.ds(pl.multiple_of(ch * half, half), half)
    other = pl.ds(pl.multiple_of(oc * half, half), half)

    load2 = pltpu.make_async_copy(w2_hbm, w2, load_sem.at[0])
    load1 = pltpu.make_async_copy(w1_hbm, w1, load_sem.at[1])
    load_cot = pltpu.make_async_copy(cot_hbm, cot, load_sem.at[2])
    load_pool = pltpu.make_async_copy(pool_hbm, pool, load_sem.at[3])
    load_cot.start()
    load_pool.start()
    load2.start()
    load1.start()

    barrier = pltpu.get_barrier_semaphore()
    for k in range(1, n):
        pl.semaphore_signal(
            barrier, inc=1, device_id={"tm": lax.rem(me + k, n)}, device_id_type=MESH
        )
    pl.semaphore_signal(barrier, inc=1, device_id={"chan": oc}, device_id_type=MESH)

    def send(index, src, dst, device):
        return pltpu.make_async_remote_copy(
            src_ref=src, dst_ref=dst, send_sem=send_sem.at[index], recv_sem=recv_sem.at[index],
            device_id=device, device_id_type=MESH,
        )

    def sums(index):
        return [
            pltpu.make_async_remote_copy(
                src_ref=stat.at[index], dst_ref=slots.at[index, k],
                send_sem=st_send.at[index], recv_sem=st_recv.at[index],
                device_id={"tm": lax.rem(me + k, n)}, device_id_type=MESH,
            )
            for k in range(1, n)
        ]

    def all_sums(index):
        block = slots.at[index, pl.ds(1, n - 1)]
        return pltpu.make_async_remote_copy(
            src_ref=block, dst_ref=block, send_sem=st_send.at[index], recv_sem=st_recv.at[index],
            device_id={"tm": after}, device_id_type=MESH,
        )

    def start_sums(index, first, second):
        pieces = [v[:, 128 * i : 128 * i + 128] for v in (first, second) for i in range(blocks)]
        pieces.append(jnp.zeros((8 - len(pieces), 128), F32))
        stat[index] = jnp.concatenate(pieces, axis=0)
        for copy in sums(index):
            copy.start()

    def finish_sums(index):
        all_sums(index).wait_recv()
        total = stat[index]
        for k in range(1, n):
            total = total + slots[index, k]
        return total

    in_group = (
        lax.broadcasted_iota(jnp.int32, (half, half), 0) // per_group
        == lax.broadcasted_iota(jnp.int32, (half, half), 1) // per_group
    ).astype(F32).astype(BF16)
    count = per_group * rows * n

    def group_means(total):
        first = jnp.concatenate([total[i : i + 1] for i in range(blocks)], axis=1)
        second = jnp.concatenate([total[blocks + i : blocks + i + 1] for i in range(blocks)], axis=1)
        both = jnp.concatenate([first, second, jnp.zeros((6, half), F32)], axis=0)
        high = both.astype(BF16).astype(F32)
        middle = (both - high).astype(BF16).astype(F32)
        parts = jnp.concatenate([high, middle, both - high - middle, jnp.zeros_like(both)], axis=0)
        spread = jnp.dot(parts.astype(BF16), in_group, preferred_element_type=F32)
        spread = (spread[0:8] + spread[8:16] + spread[16:24]) / count
        return spread[0:1], spread[1:2]

    def norm_of(total):
        mean, square = group_means(total)
        return mean, lax.rsqrt(square - mean * mean + EPS)

    def frame(ref, t):
        return ref[t * CELLS : (t + 1) * CELLS, :]

    early, late = pl.ds(0, rows - 2 * CELLS), pl.ds(rows - 2 * CELLS, 2 * CELLS)
    tail = x_ref.at[late]
    features_late = send(9, tail, fo.at[late], {"chan": oc})
    features = send(0, x_ref.at[early], fo.at[early], {"chan": oc})
    halo_mine = send(1, tail, hm, {"tm": after})
    halo_other = send(2, fo.at[late], ho, {"tm": after})
    halo_cot = send(3, wt.at[pl.ds(0, 2)], wh, {"tm": before})
    first = jnp.zeros((1, half), F32)
    second = jnp.zeros((1, half), F32)
    for t in range(frames):
        values = frame(x_ref, t).astype(F32)
        first = first + jnp.sum(values, axis=0, keepdims=True)
        second = second + jnp.sum(values * values, axis=0, keepdims=True)

    pl.semaphore_wait(barrier, n)
    features_late.start()
    start_sums(0, first, second)
    halo_mine.start()
    features.start()

    span = (2 * H1 + 1) * W1
    fast = 2 * frames
    lanes = wt.shape[1]
    frame_row = lax.broadcasted_iota(jnp.int32, (fast, 1), 0)
    scale = jnp.zeros((fast, 1), F32)
    for t in range(fast):
        scale = jnp.where(frame_row == t, fw_ref[t].astype(F32) / 4.0, scale)
    load_cot.wait()
    chunk = 16 * fast
    for i in range(lanes // 16):
        where = slice(i * chunk, (i + 1) * chunk)
        values = cot[where, :].astype(F32).reshape(16, fast, 4 * CELLS) * scale[None]
        values = values.reshape(chunk, 4 * CELLS)
        for j in range(4 * CELLS // 128):
            fine[j, where, :] = values[:, 128 * j : 128 * j + 128]
    for t in range(fast):
        for j in range(4 * CELLS // 128):
            values = fine[j, pl.ds(t, lanes, stride=fast), :]
            wt[t, :, 128 * j : 128 * j + 128] = values.astype(BF16)
        if t == 1:
            halo_cot.start()

    def keep(ref, t, values):
        for kx in range(3):
            ref[t, :, kx * lanes : (kx + 1) * lanes] = values[kx * span : (kx + 1) * span].astype(BF16)

    def pooled(values):
        both = lax.dot_general(
            pool[...], values.reshape(2 * lanes, 4 * CELLS), NT, preferred_element_type=F32
        )
        return both[:, :lanes], both[:, lanes:]

    load_pool.wait()
    for t in range(frames):
        one, two = pooled(wt[2 * t : 2 * t + 2])
        keep(even, t, one + two)
        if t > 0:
            keep(odd, t - 1, prev[...] + one)
        prev[...] = two
    halo_cot.wait()
    more = jnp.where(me < n - 1, 1.0, 0.0)
    one, two = pooled(wh[...])
    keep(even, frames, (one + two) * more)
    keep(odd, frames - 1, prev[...] + one * more)

    tot1[...] = finish_sums(0)
    partner = send(4, tot1, part1, {"chan": oc})
    partner.start()

    cell = lax.broadcasted_iota(jnp.int32, (CELLS, CELLS), 0)
    source = lax.broadcasted_iota(jnp.int32, (CELLS, CELLS), 1)
    left_of = ((source == cell - 1) & (cell % W1 > 0)).astype(F32).astype(BF16)
    right_of = ((source == cell + 1) & (cell % W1 < W1 - 1)).astype(F32).astype(BF16)

    def shifted(values):
        return (
            jnp.dot(left_of, values, preferred_element_type=F32).astype(BF16),
            values,
            jnp.dot(right_of, values, preferred_element_type=F32).astype(BF16),
        )

    inside = slice(W1, W1 + CELLS)
    for ref in (act_m, act_o, grad):
        edge = jnp.zeros((frames + 2, W1, ref.shape[2]), BF16)
        ref[:, :W1, :] = edge
        ref[:, W1 + CELLS :, :] = edge

    def activate(values, mean, inv, which):
        pre = (values.astype(F32) - mean) * inv * g1_ref[:, which] + s1_ref[:, which]
        return pre * sigmoid(pre)

    def place(ref, t, values):
        for kx, moved in enumerate(shifted(values.astype(BF16))):
            ref[t, inside, kx * half : (kx + 1) * half] = moved

    started = jnp.where(me > 0, 1.0, 0.0)
    mean1, inv1 = norm_of(tot1[...])
    features_late.wait()
    halo_other.start()
    gain1, shift1 = g1_ref[:, mine], s1_ref[:, mine]
    acc[...] = jnp.zeros_like(acc)
    for t in range(frames):
        place(act_m, t + 2, activate(frame(x_ref, t), mean1, inv1, mine))
    halo_mine.wait()
    for t in range(2):
        place(act_m, t, activate(frame(hm, t), mean1, inv1, mine) * started)
    load1.wait()

    def conv_two(which):
        low[...] = jnp.zeros_like(low)
        for kt in range(3):
            source, t0 = ((even, 1), (odd, 0), (even, 0))[kt]
            for ky in range(3):
                start = (CELLS + W1, 0, CELLS)[ky]
                left = source[t0 : t0 + frames, start : start + CELLS, :].reshape(rows, 3 * lanes)
                tap = 9 * kt + 3 * ky
                right = jnp.concatenate([w2[tap + kx, which, :] for kx in range(3)], axis=1)
                low[...] += lax.dot_general(left, right, NT, preferred_element_type=F32)

    load2.wait()
    conv_two(other)
    p2_send[...] = low[...].astype(BF16)
    exchange2 = send(5, p2_send, p2_recv, {"chan": oc})
    exchange2.start()

    partner.wait()
    mean_o, inv_o = norm_of(part1[...])
    features.wait()
    for t in range(frames):
        place(act_o, t + 2, activate(frame(fo, t), mean_o, inv_o, other))
    halo_other.wait()
    for t in range(2):
        place(act_o, t, activate(frame(ho, t), mean_o, inv_o, other) * started)
    def forward_both(kt, _):
        for ky in range(3):
            tap = 9 * kt + 3 * ky
            pieces = [
                ref[pl.ds(kt, frames), ky * W1 : ky * W1 + CELLS, :].reshape(rows, 3 * half)
                for ref in (act_m, act_o)
            ]
            weights = [w1[tap + kx, which, :] for which in (mine, other) for kx in range(3)]
            acc[...] += jnp.dot(
                jnp.concatenate(pieces, axis=1), jnp.concatenate(weights, axis=0),
                preferred_element_type=F32,
            )
        return 0

    lax.fori_loop(0, 3, forward_both, 0)
    first = jnp.zeros((1, half), F32)
    second = jnp.zeros((1, half), F32)
    for t in range(frames):
        values = (frame(acc, t) + b1_ref[...]).astype(BF16)
        hid[t * CELLS : (t + 1) * CELLS, :] = values
        values = values.astype(F32)
        first = first + jnp.sum(values, axis=0, keepdims=True)
        second = second + jnp.sum(values * values, axis=0, keepdims=True)
    start_sums(1, first, second)
    conv_two(mine)
    exchange2.wait()

    mean2, inv2 = norm_of(finish_sums(1))
    gain2, shift2 = g2_ref[:, mine], s2_ref[:, mine]

    def slope(pre):
        sig = sigmoid(pre)
        return sig * (1.0 + pre * (1.0 - sig))

    first = jnp.zeros((1, half), F32)
    second = jnp.zeros((1, half), F32)
    for t in range(frames):
        norm = (frame(hid, t).astype(F32) - mean2) * inv2
        block = frame(low, t) + frame(p2_recv, t).astype(F32)
        values = block * (slope(norm * gain2 + shift2) * gain2)
        low[t * CELLS : (t + 1) * CELLS, :] = values
        first = first + jnp.sum(values, axis=0, keepdims=True)
        second = second + jnp.sum(values * norm, axis=0, keepdims=True)
    start_sums(2, first, second)

    def norm_one(t):
        return (frame(x_ref, t).astype(F32) - mean1) * inv1

    def norm_other(t):
        return (frame(fo, t).astype(F32) - mean_o) * inv_o

    gain_o, shift_o = g1_ref[:, other], s1_ref[:, other]
    for t in range(frames):
        part = slice(t * CELLS, (t + 1) * CELLS)
        slope_m[part, :] = slope(norm_one(t) * gain1 + shift1) * gain1
        slope_o[part, :] = slope(norm_other(t) * gain_o + shift_o) * gain_o
    m1, m2 = group_means(finish_sums(2))

    def put(t, values):
        moved = shifted(values)
        for kx in range(3):
            grad[t, inside, kx * half : (kx + 1) * half] = moved[2 - kx]

    def hidden_grad(t):
        norm = (frame(hid, t).astype(F32) - mean2) * inv2
        return ((frame(low, t) - m1 - norm * m2) * inv2).astype(BF16)

    for t in range(2):
        gh[t] = hidden_grad(t)
    halo_grad = send(6, gh.at[pl.ds(0, 2)], gh.at[pl.ds(2, 2)], {"tm": before})
    halo_grad.start()
    for t in range(frames):
        put(t, gh[t] if t < 2 else hidden_grad(t))

    def back(t0, count, which):
        part = pl.ds(t0 * CELLS, count * CELLS)
        total = jnp.zeros((count * CELLS, half), F32)
        acc[part, :] = total

        def add(kt, _):
            for ky in range(3):
                y0 = (2 - ky) * W1
                left = grad[pl.ds(t0 + 2 - kt, count), y0 : y0 + CELLS, :]
                tap = 9 * kt + 3 * ky
                right = jnp.concatenate([w1[tap + kx, which, :] for kx in range(3)], axis=1)
                acc[part, :] += lax.dot_general(
                    left.reshape(count * CELLS, 3 * half), right, NT, preferred_element_type=F32
                )
            return 0

        lax.fori_loop(0, 3, add, 0)

    def send_back(index, t0, count):
        part = pl.ds(t0 * CELLS, count * CELLS)
        p1_send[part, :] = acc[part, :].astype(BF16)
        copy = send(index, p1_send.at[part], p1_recv.at[part], {"chan": oc})
        copy.start()
        return copy

    back(0, frames - 2, other)
    exchange1 = [send_back(7, 0, frames - 2)]
    halo_grad.wait()
    for t in range(2):
        put(frames + t, (gh[2 + t].astype(F32) * more).astype(BF16))
    back(frames - 2, 2, other)
    exchange1.append(send_back(10, frames - 2, 2))

    def slope_sums(slopes, norm_at):
        first = jnp.zeros((1, half), F32)
        second = jnp.zeros((1, half), F32)
        for t in range(frames):
            values = frame(acc, t) * frame(slopes, t)
            first = first + jnp.sum(values, axis=0, keepdims=True)
            second = second + jnp.sum(values * norm_at(t), axis=0, keepdims=True)
        return first, second

    start_sums(3, *slope_sums(slope_o, norm_other))
    back(0, frames, mine)
    start_sums(4, *slope_sums(slope_m, norm_one))
    tot4[...] = finish_sums(3)
    partner4 = send(8, tot4, part4, {"chan": oc})
    partner4.start()
    total = finish_sums(4)
    partner4.wait()
    m1, m2 = group_means(total + part4[...])
    for copy in exchange1:
        copy.wait()
    for t in range(frames):
        values = (frame(acc, t) + frame(p1_recv, t).astype(F32)) * frame(slope_m, t)
        values = (values - m1 - norm_one(t) * m2) * inv1
        out_ref[t * CELLS : (t + 1) * CELLS, :] = values.astype(BF16)
    for index in range(5):
        all_sums(index).wait_send()


def body(
    features, gain_one, shift_one, conv_one, bias_one, gain_two, shift_two, conv_two, cotangent,
    frame_weight,
):
    half, frames, cells = features.shape
    outs = cotangent.shape[0]
    n = lax.axis_size("tm")
    rows = frames * cells
    across = jnp.transpose(features, (1, 2, 0)).reshape(rows, half)
    fine = cotangent.reshape(outs * cotangent.shape[1], cotangent.shape[2])
    pool = pooling()
    span = pool.shape[0] // 3
    vmem = pl.BlockSpec(memory_space=pltpu.VMEM)
    hbm = pl.BlockSpec(memory_space=pl.ANY)
    out = pl.pallas_call(
        functools.partial(kernel, n, frames),
        out_shape=jax.ShapeDtypeStruct((rows, half), BF16),
        in_specs=[vmem, pl.BlockSpec(memory_space=pltpu.SMEM)] + [vmem] * 5 + [hbm] * 4,
        out_specs=vmem,
        scratch_shapes=[
            pltpu.VMEM(fine.shape, BF16),
            pltpu.VMEM((4 * cells // 128, fine.shape[0], 128), F32),
            pltpu.VMEM((2 * frames, outs, 4 * cells), BF16),
            pltpu.VMEM(pool.shape, BF16),
            pltpu.VMEM((pool.shape[0], outs), F32),
            pltpu.VMEM(conv_one.shape, BF16),
            pltpu.VMEM(conv_two.shape, BF16),
            pltpu.VMEM((rows, half), BF16),
            pltpu.VMEM((2 * cells, half), BF16),
            pltpu.VMEM((2 * cells, half), BF16),
            pltpu.VMEM((2, outs, 4 * cells), BF16),
            pltpu.VMEM((frames + 1, span, 3 * outs), BF16),
            pltpu.VMEM((frames, span, 3 * outs), BF16),
            pltpu.VMEM((rows, half), BF16),
            pltpu.VMEM((rows, half), BF16),
            pltpu.VMEM((frames + 2, cells + 2 * W1, 3 * half), BF16),
            pltpu.VMEM((frames + 2, cells + 2 * W1, 3 * half), BF16),
            pltpu.VMEM((rows, half), BF16),
            pltpu.VMEM((rows, half), F32),
            pltpu.VMEM((frames + 2, cells + 2 * W1, 3 * half), BF16),
            pltpu.VMEM((4, cells, half), BF16),
            pltpu.VMEM((rows, half), BF16),
            pltpu.VMEM((rows, half), BF16),
            pltpu.VMEM((rows, half), F32),
            pltpu.VMEM((rows, half), F32),
            pltpu.VMEM((rows, half), F32),
            pltpu.VMEM((5, 8, 128), F32),
            pltpu.VMEM((5, n, 8, 128), F32),
            pltpu.VMEM((8, 128), F32),
            pltpu.VMEM((8, 128), F32),
            pltpu.VMEM((8, 128), F32),
            pltpu.VMEM((8, 128), F32),
            pltpu.SemaphoreType.DMA((4,)),
            pltpu.SemaphoreType.DMA((11,)),
            pltpu.SemaphoreType.DMA((11,)),
            pltpu.SemaphoreType.DMA((5,)),
            pltpu.SemaphoreType.DMA((5,)),
        ],
        compiler_params=pltpu.CompilerParams(
            collective_id=0, has_side_effects=True, vmem_limit_bytes=56 * 1024 * 1024
        ),
    )(
        across, frame_weight, gain_one[None], shift_one[None], bias_one[None], gain_two[None],
        shift_two[None], fine, pool, conv_one, conv_two,
    )
    return jnp.transpose(out.reshape(frames, cells, half), (2, 0, 1))


def solution(mesh):
    placed = (
        P("chan", "tm", None),
        P(),
        P(),
        P(None, None, "chan"),
        P("chan"),
        P(),
        P(),
        P(None, None, "chan"),
        P("chan", "tm", None),
        P("tm"),
    )
    return jax.shard_map(
        body, mesh=mesh, in_specs=placed, out_specs=P("chan", "tm", None), check_vma=False
    )
```

```python
import functools

import jax
import jax.numpy as jnp
import numpy as np
from jax import lax
from jax.experimental import pallas as pl
from jax.experimental.pallas import tpu as pltpu
from jax.sharding import PartitionSpec as P

GROUPS = 32
H1 = 8
W1 = 16
CELLS = H1 * W1
EPS = 1e-06
MESH = pl.DeviceIdType.MESH
F32 = jnp.float32
BF16 = jnp.bfloat16
NT = (((1,), (1,)), ((), ()))


def pooling():
    row = np.arange(3 * (2 * H1 + 1) * W1)
    kx, q = row // ((2 * H1 + 1) * W1), row % ((2 * H1 + 1) * W1)
    odd = q >= CELLS
    y0 = np.where(odd, 2 * (q // W1 - H1) - 1, 2 * (q // W1))
    x0 = 2 * (q % W1) + 1 - kx
    fine = np.arange(4 * CELLS)
    down = fine[None] // (2 * W1) - y0[:, None]
    across = fine[None] % (2 * W1) - x0[:, None]
    hit = (down >= 0) & (down <= 1) & (across >= 0) & (across <= 1)
    return jnp.asarray(hit.astype(np.float32), dtype=BF16)


def sigmoid(values):
    return 1.0 / (1.0 + jnp.exp(-values))


def kernel(
    n, frames,
    x_ref, fw_ref, g1_ref, s1_ref, b1_ref, g2_ref, s2_ref, cot_hbm, pool_hbm, w1_hbm, w2_hbm,
    out_ref,
    cot, fine, wt, pool, prev, w1, w2, fo, hm, ho, wh, even, odd, p2_send, p2_recv, act_m, act_o, hid, low, grad, gh, p1_send, p1_recv,
    acc, slope_m, slope_o, stat, slots, tot1, part1, tot4, part4,
    load_sem, send_sem, recv_sem, st_send, st_recv,
):
    me = lax.axis_index("tm")
    ch = lax.axis_index("chan")
    oc = 1 - ch
    rows = frames * CELLS
    half = x_ref.shape[1]
    blocks = half // 128
    per_group = 2 * half // GROUPS
    after, before = lax.rem(me + 1, n), lax.rem(me + n - 1, n)
    mine = pl.ds(pl.multiple_of(ch * half, half), half)
    other = pl.ds(pl.multiple_of(oc * half, half), half)

    load2 = pltpu.make_async_copy(w2_hbm, w2, load_sem.at[0])
    load1 = pltpu.make_async_copy(w1_hbm, w1, load_sem.at[1])
    load_cot = pltpu.make_async_copy(cot_hbm, cot, load_sem.at[2])
    load_pool = pltpu.make_async_copy(pool_hbm, pool, load_sem.at[3])
    load_cot.start()
    load_pool.start()
    load2.start()
    load1.start()

    barrier = pltpu.get_barrier_semaphore()
    for k in range(1, n):
        pl.semaphore_signal(
            barrier, inc=1, device_id={"tm": lax.rem(me + k, n)}, device_id_type=MESH
        )
    pl.semaphore_signal(barrier, inc=1, device_id={"chan": oc}, device_id_type=MESH)

    def send(index, src, dst, device):
        return pltpu.make_async_remote_copy(
            src_ref=src, dst_ref=dst, send_sem=send_sem.at[index], recv_sem=recv_sem.at[index],
            device_id=device, device_id_type=MESH,
        )

    def sums(index):
        return [
            pltpu.make_async_remote_copy(
                src_ref=stat.at[index], dst_ref=slots.at[index, k],
                send_sem=st_send.at[index], recv_sem=st_recv.at[index],
                device_id={"tm": lax.rem(me + k, n)}, device_id_type=MESH,
            )
            for k in sorted(range(1, n), key=lambda k: abs(k - n // 2))
        ]

    def all_sums(index):
        block = slots.at[index, pl.ds(1, n - 1)]
        return pltpu.make_async_remote_copy(
            src_ref=block, dst_ref=block, send_sem=st_send.at[index], recv_sem=st_recv.at[index],
            device_id={"tm": after}, device_id_type=MESH,
        )

    def start_sums(index, first, second):
        pieces = [v[:, 128 * i : 128 * i + 128] for v in (first, second) for i in range(blocks)]
        pieces.append(jnp.zeros((8 - len(pieces), 128), F32))
        stat[index] = jnp.concatenate(pieces, axis=0)
        for copy in sums(index):
            copy.start()

    def finish_sums(index):
        all_sums(index).wait_recv()
        total = stat[index]
        for k in range(1, n):
            total = total + slots[index, k]
        return total

    in_group = (
        lax.broadcasted_iota(jnp.int32, (half, half), 0) // per_group
        == lax.broadcasted_iota(jnp.int32, (half, half), 1) // per_group
    ).astype(F32).astype(BF16)
    count = per_group * rows * n

    def group_means(total):
        first = jnp.concatenate([total[i : i + 1] for i in range(blocks)], axis=1)
        second = jnp.concatenate([total[blocks + i : blocks + i + 1] for i in range(blocks)], axis=1)
        both = jnp.concatenate([first, second, jnp.zeros((6, half), F32)], axis=0)
        high = both.astype(BF16).astype(F32)
        middle = (both - high).astype(BF16).astype(F32)
        parts = jnp.concatenate([high, middle, both - high - middle, jnp.zeros_like(both)], axis=0)
        spread = jnp.dot(parts.astype(BF16), in_group, preferred_element_type=F32)
        spread = (spread[0:8] + spread[8:16] + spread[16:24]) / count
        return spread[0:1], spread[1:2]

    def norm_of(total):
        mean, square = group_means(total)
        return mean, lax.rsqrt(square - mean * mean + EPS)

    def frame(ref, t):
        return ref[t * CELLS : (t + 1) * CELLS, :]

    early, late = pl.ds(0, rows - 2 * CELLS), pl.ds(rows - 2 * CELLS, 2 * CELLS)
    tail = x_ref.at[late]
    features_late = send(9, tail, fo.at[late], {"chan": oc})
    features = send(0, x_ref.at[early], fo.at[early], {"chan": oc})
    halo_mine = send(1, tail, hm, {"tm": after})
    halo_other = send(2, fo.at[late], ho, {"tm": after})
    halo_cot = send(3, wt.at[pl.ds(0, 2)], wh, {"tm": before})
    first = jnp.zeros((1, half), F32)
    second = jnp.zeros((1, half), F32)
    for t in range(frames):
        values = frame(x_ref, t).astype(F32)
        first = first + jnp.sum(values, axis=0, keepdims=True)
        second = second + jnp.sum(values * values, axis=0, keepdims=True)

    pl.semaphore_wait(barrier, n)
    features_late.start()
    start_sums(0, first, second)
    halo_mine.start()
    features.start()

    span = (2 * H1 + 1) * W1
    fast = 2 * frames
    lanes = wt.shape[1]
    frame_row = lax.broadcasted_iota(jnp.int32, (fast, 1), 0)
    scale = jnp.zeros((fast, 1), F32)
    for t in range(fast):
        scale = jnp.where(frame_row == t, fw_ref[t].astype(F32) / 4.0, scale)
    load_cot.wait()
    chunk = 16 * fast
    for i in range(lanes // 16):
        where = slice(i * chunk, (i + 1) * chunk)
        values = cot[where, :].astype(F32).reshape(16, fast, 4 * CELLS) * scale[None]
        values = values.reshape(chunk, 4 * CELLS)
        for j in range(4 * CELLS // 128):
            fine[j, where, :] = values[:, 128 * j : 128 * j + 128]
    for t in range(fast):
        for j in range(4 * CELLS // 128):
            values = fine[j, pl.ds(t, lanes, stride=fast), :]
            wt[t, :, 128 * j : 128 * j + 128] = values.astype(BF16)
        if t == 1:
            halo_cot.start()

    def keep(ref, t, values):
        for kx in range(3):
            ref[t, :, kx * lanes : (kx + 1) * lanes] = values[kx * span : (kx + 1) * span].astype(BF16)

    def pooled(values):
        both = lax.dot_general(
            pool[...], values.reshape(2 * lanes, 4 * CELLS), NT, preferred_element_type=F32
        )
        return both[:, :lanes], both[:, lanes:]

    load_pool.wait()
    for t in range(frames):
        one, two = pooled(wt[2 * t : 2 * t + 2])
        keep(even, t, one + two)
        if t > 0:
            keep(odd, t - 1, prev[...] + one)
        prev[...] = two
    halo_cot.wait()
    more = jnp.where(me < n - 1, 1.0, 0.0)
    one, two = pooled(wh[...])
    keep(even, frames, (one + two) * more)
    keep(odd, frames - 1, prev[...] + one * more)

    tot1[...] = finish_sums(0)
    partner = send(4, tot1, part1, {"chan": oc})
    partner.start()

    cell = lax.broadcasted_iota(jnp.int32, (CELLS, CELLS), 0)
    source = lax.broadcasted_iota(jnp.int32, (CELLS, CELLS), 1)
    left_of = ((source == cell - 1) & (cell % W1 > 0)).astype(F32).astype(BF16)
    right_of = ((source == cell + 1) & (cell % W1 < W1 - 1)).astype(F32).astype(BF16)

    def shifted(values):
        return (
            jnp.dot(left_of, values, preferred_element_type=F32).astype(BF16),
            values,
            jnp.dot(right_of, values, preferred_element_type=F32).astype(BF16),
        )

    inside = slice(W1, W1 + CELLS)
    for ref in (act_m, act_o, grad):
        edge = jnp.zeros((frames + 2, W1, ref.shape[2]), BF16)
        ref[:, :W1, :] = edge
        ref[:, W1 + CELLS :, :] = edge

    def activate(values, mean, inv, which):
        pre = (values.astype(F32) - mean) * inv * g1_ref[:, which] + s1_ref[:, which]
        return pre * sigmoid(pre)

    def place(ref, t, values):
        for kx, moved in enumerate(shifted(values.astype(BF16))):
            ref[t, inside, kx * half : (kx + 1) * half] = moved

    started = jnp.where(me > 0, 1.0, 0.0)
    mean1, inv1 = norm_of(tot1[...])
    features_late.wait()
    halo_other.start()
    gain1, shift1 = g1_ref[:, mine], s1_ref[:, mine]
    acc[...] = jnp.zeros_like(acc)
    for t in range(frames):
        place(act_m, t + 2, activate(frame(x_ref, t), mean1, inv1, mine))
    halo_mine.wait()
    for t in range(2):
        place(act_m, t, activate(frame(hm, t), mean1, inv1, mine) * started)
    load1.wait()

    def conv_two(which):
        low[...] = jnp.zeros_like(low)
        for kt in range(3):
            source, t0 = ((even, 1), (odd, 0), (even, 0))[kt]
            for ky in range(3):
                start = (CELLS + W1, 0, CELLS)[ky]
                left = source[t0 : t0 + frames, start : start + CELLS, :].reshape(rows, 3 * lanes)
                tap = 9 * kt + 3 * ky
                right = jnp.concatenate([w2[tap + kx, which, :] for kx in range(3)], axis=1)
                low[...] += lax.dot_general(left, right, NT, preferred_element_type=F32)

    load2.wait()
    conv_two(other)
    p2_send[...] = low[...].astype(BF16)
    exchange2 = send(5, p2_send, p2_recv, {"chan": oc})
    exchange2.start()

    partner.wait()
    mean_o, inv_o = norm_of(part1[...])
    features.wait()
    for t in range(frames):
        place(act_o, t + 2, activate(frame(fo, t), mean_o, inv_o, other))
    halo_other.wait()
    for t in range(2):
        place(act_o, t, activate(frame(ho, t), mean_o, inv_o, other) * started)
    def forward_both(kt, _):
        for ky in range(3):
            tap = 9 * kt + 3 * ky
            pieces = [
                ref[pl.ds(kt, frames), ky * W1 : ky * W1 + CELLS, :].reshape(rows, 3 * half)
                for ref in (act_m, act_o)
            ]
            weights = [w1[tap + kx, which, :] for which in (mine, other) for kx in range(3)]
            acc[...] += jnp.dot(
                jnp.concatenate(pieces, axis=1), jnp.concatenate(weights, axis=0),
                preferred_element_type=F32,
            )
        return 0

    lax.fori_loop(0, 3, forward_both, 0)
    first = jnp.zeros((1, half), F32)
    second = jnp.zeros((1, half), F32)
    for t in range(frames):
        values = (frame(acc, t) + b1_ref[...]).astype(BF16)
        hid[t * CELLS : (t + 1) * CELLS, :] = values
        values = values.astype(F32)
        first = first + jnp.sum(values, axis=0, keepdims=True)
        second = second + jnp.sum(values * values, axis=0, keepdims=True)
    start_sums(1, first, second)
    conv_two(mine)
    exchange2.wait()

    mean2, inv2 = norm_of(finish_sums(1))
    gain2, shift2 = g2_ref[:, mine], s2_ref[:, mine]

    def slope(pre):
        sig = sigmoid(pre)
        return sig * (1.0 + pre * (1.0 - sig))

    first = jnp.zeros((1, half), F32)
    second = jnp.zeros((1, half), F32)
    for t in range(frames):
        norm = (frame(hid, t).astype(F32) - mean2) * inv2
        block = frame(low, t) + frame(p2_recv, t).astype(F32)
        values = block * (slope(norm * gain2 + shift2) * gain2)
        low[t * CELLS : (t + 1) * CELLS, :] = values
        first = first + jnp.sum(values, axis=0, keepdims=True)
        second = second + jnp.sum(values * norm, axis=0, keepdims=True)
    start_sums(2, first, second)

    def norm_one(t):
        return (frame(x_ref, t).astype(F32) - mean1) * inv1

    def norm_other(t):
        return (frame(fo, t).astype(F32) - mean_o) * inv_o

    gain_o, shift_o = g1_ref[:, other], s1_ref[:, other]
    for t in range(frames):
        part = slice(t * CELLS, (t + 1) * CELLS)
        slope_m[part, :] = slope(norm_one(t) * gain1 + shift1) * gain1
        slope_o[part, :] = slope(norm_other(t) * gain_o + shift_o) * gain_o
    m1, m2 = group_means(finish_sums(2))

    def put(t, values):
        moved = shifted(values)
        for kx in range(3):
            grad[t, inside, kx * half : (kx + 1) * half] = moved[2 - kx]

    def hidden_grad(t):
        norm = (frame(hid, t).astype(F32) - mean2) * inv2
        return ((frame(low, t) - m1 - norm * m2) * inv2).astype(BF16)

    for t in range(2):
        gh[t] = hidden_grad(t)
    halo_grad = send(6, gh.at[pl.ds(0, 2)], gh.at[pl.ds(2, 2)], {"tm": before})
    halo_grad.start()
    for t in range(frames):
        put(t, gh[t] if t < 2 else hidden_grad(t))

    def back(t0, count, which):
        part = pl.ds(t0 * CELLS, count * CELLS)
        total = jnp.zeros((count * CELLS, half), F32)
        acc[part, :] = total

        def add(kt, _):
            for ky in range(3):
                y0 = (2 - ky) * W1
                left = grad[pl.ds(t0 + 2 - kt, count), y0 : y0 + CELLS, :]
                tap = 9 * kt + 3 * ky
                right = jnp.concatenate([w1[tap + kx, which, :] for kx in range(3)], axis=1)
                acc[part, :] += lax.dot_general(
                    left.reshape(count * CELLS, 3 * half), right, NT, preferred_element_type=F32
                )
            return 0

        lax.fori_loop(0, 3, add, 0)

    def send_back(index, t0, count):
        part = pl.ds(t0 * CELLS, count * CELLS)
        p1_send[part, :] = acc[part, :].astype(BF16)
        copy = send(index, p1_send.at[part], p1_recv.at[part], {"chan": oc})
        copy.start()
        return copy

    back(0, frames - 2, other)
    exchange1 = [send_back(7, 0, frames - 2)]
    halo_grad.wait()
    for t in range(2):
        put(frames + t, (gh[2 + t].astype(F32) * more).astype(BF16))
    back(frames - 2, 2, other)
    exchange1.append(send_back(10, frames - 2, 2))

    def slope_sums(slopes, norm_at):
        first = jnp.zeros((1, half), F32)
        second = jnp.zeros((1, half), F32)
        for t in range(frames):
            values = frame(acc, t) * frame(slopes, t)
            first = first + jnp.sum(values, axis=0, keepdims=True)
            second = second + jnp.sum(values * norm_at(t), axis=0, keepdims=True)
        return first, second

    start_sums(3, *slope_sums(slope_o, norm_other))
    back(0, frames, mine)
    start_sums(4, *slope_sums(slope_m, norm_one))
    tot4[...] = finish_sums(3)
    partner4 = send(8, tot4, part4, {"chan": oc})
    partner4.start()
    total = finish_sums(4)
    partner4.wait()
    m1, m2 = group_means(total + part4[...])
    for copy in exchange1:
        copy.wait()
    for t in range(frames):
        values = (frame(acc, t) + frame(p1_recv, t).astype(F32)) * frame(slope_m, t)
        values = (values - m1 - norm_one(t) * m2) * inv1
        out_ref[t * CELLS : (t + 1) * CELLS, :] = values.astype(BF16)
    for index in range(5):
        all_sums(index).wait_send()


def body(
    features, gain_one, shift_one, conv_one, bias_one, gain_two, shift_two, conv_two, cotangent,
    frame_weight,
):
    half, frames, cells = features.shape
    outs = cotangent.shape[0]
    n = lax.axis_size("tm")
    rows = frames * cells
    across = jnp.transpose(features, (1, 2, 0)).reshape(rows, half)
    fine = cotangent.reshape(outs * cotangent.shape[1], cotangent.shape[2])
    pool = pooling()
    span = pool.shape[0] // 3
    vmem = pl.BlockSpec(memory_space=pltpu.VMEM)
    hbm = pl.BlockSpec(memory_space=pl.ANY)
    out = pl.pallas_call(
        functools.partial(kernel, n, frames),
        out_shape=jax.ShapeDtypeStruct((rows, half), BF16),
        in_specs=[vmem, pl.BlockSpec(memory_space=pltpu.SMEM)] + [vmem] * 5 + [hbm] * 4,
        out_specs=vmem,
        scratch_shapes=[
            pltpu.VMEM(fine.shape, BF16),
            pltpu.VMEM((4 * cells // 128, fine.shape[0], 128), F32),
            pltpu.VMEM((2 * frames, outs, 4 * cells), BF16),
            pltpu.VMEM(pool.shape, BF16),
            pltpu.VMEM((pool.shape[0], outs), F32),
            pltpu.VMEM(conv_one.shape, BF16),
            pltpu.VMEM(conv_two.shape, BF16),
            pltpu.VMEM((rows, half), BF16),
            pltpu.VMEM((2 * cells, half), BF16),
            pltpu.VMEM((2 * cells, half), BF16),
            pltpu.VMEM((2, outs, 4 * cells), BF16),
            pltpu.VMEM((frames + 1, span, 3 * outs), BF16),
            pltpu.VMEM((frames, span, 3 * outs), BF16),
            pltpu.VMEM((rows, half), BF16),
            pltpu.VMEM((rows, half), BF16),
            pltpu.VMEM((frames + 2, cells + 2 * W1, 3 * half), BF16),
            pltpu.VMEM((frames + 2, cells + 2 * W1, 3 * half), BF16),
            pltpu.VMEM((rows, half), BF16),
            pltpu.VMEM((rows, half), F32),
            pltpu.VMEM((frames + 2, cells + 2 * W1, 3 * half), BF16),
            pltpu.VMEM((4, cells, half), BF16),
            pltpu.VMEM((rows, half), BF16),
            pltpu.VMEM((rows, half), BF16),
            pltpu.VMEM((rows, half), F32),
            pltpu.VMEM((rows, half), F32),
            pltpu.VMEM((rows, half), F32),
            pltpu.VMEM((5, 8, 128), F32),
            pltpu.VMEM((5, n, 8, 128), F32),
            pltpu.VMEM((8, 128), F32),
            pltpu.VMEM((8, 128), F32),
            pltpu.VMEM((8, 128), F32),
            pltpu.VMEM((8, 128), F32),
            pltpu.SemaphoreType.DMA((4,)),
            pltpu.SemaphoreType.DMA((11,)),
            pltpu.SemaphoreType.DMA((11,)),
            pltpu.SemaphoreType.DMA((5,)),
            pltpu.SemaphoreType.DMA((5,)),
        ],
        compiler_params=pltpu.CompilerParams(
            collective_id=0, has_side_effects=True, vmem_limit_bytes=56 * 1024 * 1024
        ),
    )(
        across, frame_weight, gain_one[None], shift_one[None], bias_one[None], gain_two[None],
        shift_two[None], fine, pool, conv_one, conv_two,
    )
    return jnp.transpose(out.reshape(frames, cells, half), (2, 0, 1))


def solution(mesh):
    placed = (
        P("chan", "tm", None),
        P(),
        P(),
        P(None, None, "chan"),
        P("chan"),
        P(),
        P(),
        P(None, None, "chan"),
        P("chan", "tm", None),
        P("tm"),
    )
    return jax.shard_map(
        body, mesh=mesh, in_specs=placed, out_specs=P("chan", "tm", None), check_vma=False
    )
```
